128 devices in a mesh: groups: 32 (over z, y, core), blk: 4 (over x).
Axes of the slice: x: 4, y: 4, z: 4, core: 2. Of those that a mesh axis runs over, the one named last changes fastest.
Arguments:
- embeddings: bfloat16 [98304, 1024], P(('groups', 'blk')), may hold values from -6 to 6
- owner: int32 [98304, 1], P(('groups', 'blk')), may hold values from 0 to 31; in each aligned block of 768 rows (0 to 767, 768 to 1535, ...) at most 48 rows name the same one
- local_cluster: int32 [98304], P(('groups', 'blk')), may hold values from 0 to 15
Outputs:
- best: float32 [98304], P(('groups', 'blk'))
The draws below stay inside these ranges and needn't reach their ends.
Inputs may be any that keep to these rules, and one draw needn't show every extreme that they name: `owner`: among the rows of one device no group is named by more than 48 rows, a bound that some block reaches.
All inputs are finite; a program needn't handle non-finite values.
Results may differ from the reference program's by a relative error of at most 0.0013.
Values may be sent and summed in bfloat16 or wider, within the bound.
No kernel may reach another device: no remote copies, remote signals or barrier semaphores. Data moves between devices by JAX's collectives and lax.ppermute only.
A program may use at most 64 MiB of HBM per device.

```python
import math
import jax
import jax.numpy as jnp
import numpy as np
from jax import lax

D = 1024
ROW_DEV = 768
CPG = 16
SEND_CAP = 48
ROWS = 98304
N_GROUPS = 32
N_BLK = 4


def plant(entries, own_key, smallest, high):
    index_at = [jax.random.randint(jax.random.fold_in(own_key, axis), (), 0, length) for axis, length in enumerate(entries.shape)]
    longest = entries.shape.index(max(entries.shape))
    next_to = index_at[:longest] + [(index_at[longest] + 1) % entries.shape[longest]] + index_at[longest + 1:]
    return entries.at[tuple(index_at)].set(smallest).at[tuple(next_to)].set(high)


def level_of(key, shape, pieces, smallest, high):
    factor_of = 1.0
    for dim, blocks in pieces:
        draws = jax.random.uniform(jax.random.fold_in(jax.random.fold_in(key, 6), dim), (blocks,), jnp.float32, smallest / len(pieces), high / len(pieces))
        factor_of = factor_of * jnp.repeat(jnp.exp(draws), shape[dim] // blocks).reshape((-1,) + (1,) * (len(shape) - 1 - dim))
    return factor_of


def routed_block(rng, own, number, rows, number_of, top, bound, lean):
    sequence = jax.random.permutation(rng, number_of)
    packed, common = load_shares(number_of, rows * top, bound, lean, True), load_shares(number_of, rows * top, bound, lean, False)
    places = jnp.arange(number_of)

    def named(lengths, offset_by):
        used = int((lengths > 0).sum())
        fixed = max(1, used // 4)
        passed = fixed + (places - fixed + offset_by * (used - fixed)) % max(1, number_of - fixed)
        return jnp.zeros((number_of,), jnp.int32).at[sequence[jnp.where(places < fixed, places, passed)]].set(jnp.asarray(lengths, jnp.int32))

    lengths = jnp.where(number % 4 == 0, named(packed, number // 4), named(common, number - number // 4 - 1))
    mixed = jax.random.permutation(jax.random.fold_in(own, 3), number_of)
    donor, receiver = mixed[0:number_of // 2 * 2:2], mixed[1:number_of // 2 * 2:2]
    margin = jnp.minimum(lengths[donor] - 1, bound - lengths[receiver]) // 2
    margin = jnp.where((donor == sequence[0]) | (receiver == sequence[0]) | (lengths[receiver] == 0), 0, jnp.maximum(margin, 0))
    passed = jax.random.randint(jax.random.fold_in(own, 4), (number_of // 2,), 0, 1 << 20) % (margin + 1)
    lengths = lengths.at[donor].add(-passed).at[receiver].add(passed)
    members = jnp.searchsorted(jnp.cumsum(lengths), jnp.arange(rows * top), side="right").astype(jnp.int32)
    listing = members.reshape(top, rows).T
    listing = listing[jax.random.permutation(jax.random.fold_in(own, 1), rows)]
    offset_by = jax.random.randint(jax.random.fold_in(own, 2), (rows, 1), 0, top)
    return jnp.take_along_axis(listing, (jnp.arange(top)[None, :] + offset_by) % top, axis=1)


def load_shares(amount, total, bound, slope, full):
    weights = [(1 << 20) // math.isqrt(grade ** slope) + 1 for grade in range(1, amount + 1)]
    largest = bound if full else min(bound, max(-(-total // amount), total * weights[0] // sum(weights)))
    least = 1 if total - largest >= amount - 1 else 0
    counts, spare = [largest] + [least] * (amount - 1), total - largest - least * (amount - 1)
    while spare > 0:
        free = [i for i in range(1, amount) if counts[i] < largest] or [i for i in range(1, amount) if counts[i] < bound]
        pool, remaining = sum([weights[i] for i in free]), spare
        for i in free:
            addition = min(bound - counts[i], max(1, remaining * weights[i] // pool), spare)
            counts[i] = counts[i] + addition
            spare = spare - addition
    return np.array(counts)


def centred(stream_key, dims, spread, limit, split=(), kind=jnp.bfloat16):
    entries = spread * jax.random.normal(stream_key, dims, jnp.float32)
    if split:
        entries = entries * level_of(stream_key, dims, split, -0.22, 0.18)
    return jnp.clip(entries, -limit, limit).astype(kind)


def setup_inputs(seed: int = 0) -> dict:
    key_of = jax.random.split(jax.random.key(seed), 4)
    embeddings = centred(key_of[0], (ROWS, D), 1.0, 6.0, ((0, 128),))
    owner_keys = jax.random.split(jax.random.fold_in(key_of[1], 1), ROWS // ROW_DEV)
    owner_turns = jax.random.permutation(jax.random.fold_in(key_of[1], 3), ROWS // ROW_DEV)
    owner = jax.vmap(lambda own, number: routed_block(jax.random.fold_in(key_of[1], 2), own, number, ROW_DEV, N_GROUPS, 1, SEND_CAP, 1))(owner_keys, owner_turns).reshape((ROWS, 1))
    local_cluster = plant(jax.random.randint(key_of[2], (ROWS,), 0, CPG), jax.random.fold_in(key_of[2], 1), 0, CPG - 1).astype(jnp.int32)
    return dict(embeddings=embeddings, owner=owner, local_cluster=local_cluster)


def reference(embeddings, owner, local_cluster):
    emb32 = embeddings.astype(jnp.float32)
    scale = lax.rsqrt(lax.optimization_barrier(jnp.mean(emb32 * emb32, axis=1, keepdims=True)) + 1e-06) / math.sqrt(D)
    unit = (emb32 * scale).astype(jnp.bfloat16)
    target = owner[:, 0].astype(jnp.int32)
    cluster = target * CPG + local_cluster
    group_cap = N_GROUPS * N_BLK * SEND_CAP

    def one_group(g):
        hits = target == g
        index = jnp.nonzero(hits, size=group_cap, fill_value=0)[0].astype(jnp.int32)
        valid = jnp.arange(group_cap, dtype=jnp.int32) < jnp.sum(hits.astype(jnp.int32))
        picked = unit[index].astype(jnp.float32)
        labels = jnp.where(valid, cluster[index], -1)
        prod = jnp.dot(picked, picked.T, precision=lax.Precision.HIGHEST)
        keep = (labels[:, None] == labels[None, :]) & (index[None, :] < index[:, None]) & valid[None, :] & valid[:, None]
        maxima = lax.optimization_barrier(jnp.max(jnp.where(keep, prod, -1.0), axis=1))
        return (jnp.where(valid, maxima, -1.0).astype(jnp.float32), index)
    maxima, index = lax.map(one_group, jnp.arange(N_GROUPS, dtype=jnp.int32))
    best = jnp.full((ROWS,), -1.0, jnp.float32)
    return best.at[index.reshape(-1)].max(maxima.reshape(-1))
```

```python
import math

import jax
import jax.numpy as jnp
from jax import lax
from jax.experimental import pallas as pl
from jax.experimental.pallas import tpu as pltpu
from jax.sharding import Mesh, PartitionSpec as P

CPG = 16
GROUPS = 32
CLUSTERS = GROUPS * CPG
ROWS = 768
WIDTH = 1024
CHIPS = 64
DEVS = 128
CAP = 24
SLOTS = CHIPS * CAP
ALL = ("z", "y", "core", "x")
GROUP_AXES = ("z", "y", "core")
CHIP_AXES = ("z", "y", "x")
SHIFTS = (
    (0, 0, 0), (3, 7, 12), (5, 14, 9), (11, 2, 6), (8, 4, 13), (1, 10, 3), (14, 6, 2), (7, 13, 15),
    (12, 1, 8), (2, 9, 5), (9, 15, 1), (6, 3, 11), (15, 12, 4), (4, 11, 7), (10, 5, 14), (13, 8, 10),
)
BF16 = jnp.bfloat16
F32 = jnp.float32


def iota(shape, dim):
    return lax.broadcasted_iota(jnp.int32, shape, dim)


def dot(a, b, ca=1, cb=0, precision=None):
    return lax.dot_general(
        a, b, (((ca,), (cb,)), ((), ())), preferred_element_type=F32, precision=precision
    )


def onehot(cond):
    return jnp.where(cond, 1.0, 0.0).astype(BF16)


def place():
    zy = lax.axis_index("z") * 4 + lax.axis_index("y")
    return lax.axis_index("core"), zy * 4 + lax.axis_index("x")


def count_kernel(owner_ref, local_ref, hist_ref, ids_ref):
    owner, local = owner_ref[...], local_ref[...]
    by_owner = onehot(owner == iota((GROUPS, ROWS), 0))
    by_local = onehot(local == iota((CPG, ROWS), 0))
    pairs = dot(by_owner, by_local, 1, 1).astype(BF16)
    spread = onehot(iota((CPG, CLUSTERS), 1) % CPG == iota((CPG, CLUSTERS), 0))
    wide = dot(pairs, spread)
    mine = iota((GROUPS, CLUSTERS), 1) // CPG == iota((GROUPS, CLUSTERS), 0)
    counts = jnp.sum(jnp.where(mine, wide, 0.0), axis=0, keepdims=True)
    for j in range(CLUSTERS // 128):
        part = counts[:, j * 128 : (j + 1) * 128]
        hist_ref[:, j, :] = jnp.broadcast_to(part, (DEVS, 128))
    cluster = owner * CPG + local
    eye = iota((128, 128), 0) == iota((128, 128), 1)
    rank = jnp.zeros((1, ROWS), jnp.int32)
    for j in range(ROWS // 128):
        part = jnp.broadcast_to(cluster[:, j * 128 : (j + 1) * 128], (128, 128))
        column = jnp.sum(jnp.where(eye, part, 0), axis=1, keepdims=True)
        width = ROWS - j * 128
        later = iota((128, width), 1) > iota((128, width), 0)
        hit = jnp.where((column == cluster[:, j * 128 :]) & later, 1, 0)
        found = jnp.sum(hit, axis=0, keepdims=True)
        if j:
            found = jnp.concatenate([jnp.zeros((1, j * 128), jnp.int32), found], axis=1)
        rank = rank + found
    which = iota((8, ROWS), 0)
    ids_ref[...] = jnp.where(which == 0, cluster, jnp.where(which == 1, rank, 0))


def unit_kernel(emb_ref, unit_ref):
    emb = emb_ref[...].astype(F32)
    scale = lax.rsqrt(jnp.mean(emb * emb, axis=1, keepdims=True) + 1e-06) / math.sqrt(WIDTH)
    unit_ref[...] = (emb * scale).astype(BF16)


def rotate(value, by):
    if by == 0:
        return value
    inside = iota(value.shape, 1) % 16 >= by
    return jnp.where(inside, pltpu.roll(value, by, 1), pltpu.roll(value, by + 112, 1))


def pack_kernel(hist_ref, ids_ref, ids2_ref, unit_ref, unit2_ref, out_ref, ends_ref, rows_ref, load_ref):
    core, chip = place()
    hist = jnp.concatenate([hist_ref[:, j, :] for j in range(4)], axis=1).astype(BF16)
    dev = iota((CHIPS, DEVS), 1)
    first = iota((CHIPS, DEVS), 0) // 4 * 8 + iota((CHIPS, DEVS), 0) % 4
    count0 = dot(onehot(dev == first), hist)
    count1 = dot(onehot(dev == first + 4), hist)
    both = (count0 + count1).astype(BF16)

    in_group = iota((CLUSTERS, GROUPS), 0) // CPG == iota((CLUSTERS, GROUPS), 1)
    in_group_t = iota((GROUPS, CLUSTERS), 1) // CPG == iota((GROUPS, CLUSTERS), 0)
    size_row = jnp.sum(dot(both, onehot(in_group)), axis=0, keepdims=True)
    size_col = jnp.sum(dot(onehot(in_group_t), both, 1, 1), axis=1, keepdims=True)
    lower = iota((GROUPS, GROUPS), 0) < iota((GROUPS, GROUPS), 1)
    ahead = (size_col > size_row) | ((size_col == size_row) & lower)
    order = jnp.sum(jnp.where(ahead, 1, 0), axis=0, keepdims=True)
    order = jnp.sum(jnp.where(in_group, order, 0), axis=1, keepdims=True)
    quarter = order // 8
    place8 = order % 8
    octet = jnp.where(quarter % 2 == 1, 7 - place8, place8)
    local = iota((CLUSTERS, 1), 0) % CPG
    lane = iota((CLUSTERS, CLUSTERS), 1)
    spread = onehot(quarter * 128 + octet * 16 + local == lane)

    wide = dot(both, spread)
    parts = [wide[:, p * 128 : (p + 1) * 128] for p in range(4)]
    loads = []
    for shifts in SHIFTS:
        load = parts[0]
        for part, by in zip(parts[1:], shifts):
            load = load + rotate(part, by)
        loads.append(jnp.max(load, axis=0, keepdims=True))
    loads = jnp.concatenate(loads, axis=0)
    for by in (1, 2, 4, 8):
        loads = jnp.maximum(loads, rotate(loads, by))
    best = loads[0:1]
    chosen = [jnp.full((1, 128), by, jnp.int32) for by in SHIFTS[0]]
    for n, shifts in enumerate(SHIFTS[1:], 1):
        better = loads[n : n + 1] < best
        best = jnp.where(better, loads[n : n + 1], best)
        chosen = [jnp.where(better, by, old) for by, old in zip(shifts, chosen)]
    load_ref[...] = jnp.broadcast_to(jnp.max(best, axis=1, keepdims=True), (8, 128)).astype(jnp.int32)
    chosen = jnp.concatenate([jnp.zeros((1, 128), jnp.int32)] + chosen, axis=1)
    chosen = jnp.broadcast_to(chosen, (8, CLUSTERS)).astype(F32).astype(BF16)
    shift = dot(spread, chosen, 1, 1)[:, 0:1].astype(jnp.int32)
    device = octet * 16 + (local + shift) % 16
    spread = onehot(quarter * 128 + device == lane)
    count0 = dot(count0.astype(BF16), spread)
    count1 = dot(count1.astype(BF16), spread)

    at = iota((CLUSTERS, 8), 0)
    upto = iota((CLUSTERS, 8), 1)
    mine = at % 128 == core * CHIPS + chip
    ends_ref[...] = dot(
        count0.astype(BF16), onehot(mine & (at // 128 * 2 <= upto))
    ) + dot(count1.astype(BF16), onehot(mine & (at // 128 * 2 + 1 <= upto)))

    here = iota((CHIPS, CLUSTERS), 0) == chip
    own0 = jnp.sum(jnp.where(here, count0, 0.0), axis=0, keepdims=True)
    own1 = jnp.sum(jnp.where(here, count1, 0.0), axis=0, keepdims=True)
    own = own0 + own1
    start = [jnp.zeros((1, 128), F32)]
    for p in range(3):
        start.append(start[-1] + own[:, p * 128 : (p + 1) * 128])
    start0 = jnp.concatenate(start, axis=1)
    start1 = start0 + own0
    which = iota((8, CLUSTERS), 0)
    device_row = (iota((8, CLUSTERS), 1) % 128).astype(F32)
    table = jnp.where(
        which == 0, device_row, jnp.where(which == 1, start0, jnp.where(which == 2, start1, 0.0))
    ).astype(BF16)
    table = dot(table, spread, 1, 1).astype(BF16)

    def slots(ids, of_core):
        looked = dot(table, onehot(ids[0:1] == iota((CLUSTERS, ROWS), 0)))
        looked = looked.astype(jnp.int32)
        to = looked[0:1]
        k = jnp.where(of_core == 0, looked[1:2], looked[2:3]) + ids[1:2]
        return to, k, jnp.where(to // CHIPS == core, to % CHIPS * CAP + k, -1)

    to, k, slot = slots(ids_ref[...], core)
    _, _, slot2 = slots(ids2_ref[...], 1 - core)
    which = iota((8, ROWS), 0)
    rows_ref[...] = jnp.where(which == 0, to, jnp.where(which == 1, k, 0))
    tile = 256
    for n in range(SLOTS // tile):
        at = iota((tile, ROWS), 0) + n * tile
        out_ref[n * tile : (n + 1) * tile, :] = (
            dot(onehot(slot == at), unit_ref[...]) + dot(onehot(slot2 == at), unit2_ref[...])
        ).astype(BF16)


def pairs_kernel(rows_ref, ends_ref, out_ref):
    ends = ends_ref[...].astype(BF16)

    def keys(at, past):
        chip = at * 2731 // 65536
        k = at - chip * CAP
        n = past(chip, k)
        key = ((chip // 4 * 8 + n % 2 * 4 + chip % 4) * 32) + k
        return n // 2 * 8192, n // 2 * 8192 + key

    def past_col(chip, k):
        ends_col = dot(onehot(chip == iota((SLOTS, CHIPS), 1)), ends)
        return jnp.sum(jnp.where(k.astype(F32) >= ends_col, 1, 0), axis=1, keepdims=True)

    def past_row(chip, k):
        ends_row = dot(ends, onehot(chip == iota((CHIPS, SLOTS), 0)), 0, 0)
        return jnp.sum(jnp.where(k.astype(F32) >= ends_row, 1, 0), axis=0, keepdims=True)

    _, key_col = keys(iota((SLOTS, 1), 0), past_col)
    low_row, key_row = keys(iota((1, SLOTS), 1), past_row)
    tile = 384
    best = []
    for i in range(SLOTS // tile):
        mine = slice(i * tile, (i + 1) * tile)
        top = jnp.full((1, tile), -1.0, F32)
        for j in range(i + 1):
            other = slice(j * tile, (j + 1) * tile)
            score = dot(rows_ref[other, :], rows_ref[mine, :], 1, 1)
            key = key_col[other]
            keep = (key >= low_row[:, mine]) & (key < key_row[:, mine])
            top = jnp.maximum(top, jnp.max(jnp.where(keep, score, -1.0), axis=0, keepdims=True))
        best.append(top)
    best = jnp.concatenate(best, axis=1)
    dev = iota((DEVS, SLOTS), 0)
    chip = iota((1, SLOTS), 1) * 2731 // 65536
    block = jnp.where(dev // 8 * 4 + dev % 4 == chip, best, 0.0)
    at = iota((SLOTS, 128), 0)
    column = jnp.where(at - at * 2731 // 65536 * CAP == iota((SLOTS, 128), 1), 1.0, 0.0)
    out_ref[...] = dot(block, column, precision=lax.Precision.HIGHEST)


def home_kernel(got_ref, rows_ref, out_ref):
    to, k = rows_ref[0:1, :], rows_ref[1:2, :]
    chip = to % CHIPS
    dev = chip // 4 * 8 + to // CHIPS * 4 + chip % 4
    pick = jnp.where(dev == iota((DEVS, ROWS), 0), 1.0, 0.0)
    cand = dot(got_ref[:, 0:32], pick, 0, 0, precision=lax.Precision.HIGHEST)
    best = jnp.sum(jnp.where(k == iota((32, ROWS), 0), cand, 0.0), axis=0, keepdims=True)
    for j in range(ROWS // 128):
        out_ref[j : j + 1, :] = best[:, j * 128 : (j + 1) * 128]


def call(kernel, out_shape, *args, **kwargs):
    return pl.pallas_call(
        kernel,
        out_shape=out_shape,
        compiler_params=pltpu.CompilerParams(vmem_limit_bytes=48 * 2**20),
        **kwargs,
    )(*args)


def shape(*dims, dtype=F32):
    return jax.ShapeDtypeStruct(dims, dtype)


def by_groups(embeddings, owner, local_cluster):
    rows, width = embeddings.shape
    n_groups = GROUPS
    cap = 2 * rows // n_groups
    emb32 = embeddings.astype(F32)
    scale = lax.rsqrt(jnp.mean(emb32 * emb32, axis=1, keepdims=True) + 1e-06) / math.sqrt(width)
    unit = (emb32 * scale).astype(BF16)
    target = owner[:, 0]
    cluster = target * CPG + local_cluster
    device = lax.axis_index(ALL)
    global_id = device * rows + jnp.arange(rows, dtype=jnp.int32)
    onehots = (target[:, None] == jnp.arange(n_groups, dtype=jnp.int32)[None, :]).astype(jnp.int32)
    rank = jnp.sum(jnp.cumsum(onehots, axis=0) * onehots, axis=1) - 1
    slot = target * cap + rank
    size = n_groups * cap

    def send(x, fill):
        full = jnp.full((size,) + x.shape[1:], fill, x.dtype).at[slot].set(x)
        full = full.reshape((n_groups, cap) + x.shape[1:])
        got = lax.all_to_all(full, GROUP_AXES, split_axis=0, concat_axis=0, tiled=True)
        return got.reshape((size,) + x.shape[1:])

    mine, ids, labels = send(unit, 0), send(global_id, -1), send(cluster, -1)
    rows4, ids4, labels4 = (lax.all_gather(x, "x", axis=0, tiled=True) for x in (mine, ids, labels))
    prod = jnp.einsum("id,jd->ij", mine, rows4, preferred_element_type=F32)
    keep = (labels[:, None] == labels4[None, :]) & (ids4[None, :] < ids[:, None])
    best = jnp.maximum(-1.0, jnp.max(jnp.where(keep, prod, -1.0), axis=1))
    back = lax.all_to_all(
        best.reshape(n_groups, cap), GROUP_AXES, split_axis=0, concat_axis=0, tiled=True
    )
    return back.reshape(size)[slot]


def by_devices(packed, ends, places):
    got = lax.all_to_all(
        packed.reshape(CHIPS, CAP, WIDTH), CHIP_AXES, split_axis=0, concat_axis=0, tiled=True
    )
    best = call(pairs_kernel, shape(DEVS, 128), got.reshape(SLOTS, WIDTH), ends)
    back = lax.all_to_all(best, ALL, split_axis=0, concat_axis=0, tiled=True)
    return call(home_kernel, shape(ROWS // 128, 128), back, places).reshape(ROWS)


def body(embeddings, owner, local_cluster):
    hist, ids = call(
        count_kernel,
        (shape(DEVS, 4, 128), shape(8, ROWS, dtype=jnp.int32)),
        owner.reshape(1, ROWS),
        local_cluster.reshape(1, ROWS),
    )
    hists = lax.all_to_all(hist, ALL, split_axis=0, concat_axis=0, tiled=True)
    block = pl.BlockSpec((192, WIDTH), lambda i: (i, 0))
    unit = call(
        unit_kernel,
        shape(ROWS, WIDTH, dtype=BF16),
        embeddings,
        grid=(4,),
        in_specs=[block],
        out_specs=block,
    )
    swap = [(0, 1), (1, 0)]
    unit2, ids2 = lax.ppermute(unit, "core", swap), lax.ppermute(ids, "core", swap)
    packed, ends, places, load = call(
        pack_kernel,
        (
            shape(SLOTS, WIDTH, dtype=BF16),
            shape(CHIPS, 8),
            shape(8, ROWS, dtype=jnp.int32),
            shape(8, 128, dtype=jnp.int32),
        ),
        hists, ids, ids2, unit, unit2,
    )
    return lax.cond(
        load[0, 0] <= CAP,
        lambda: by_devices(packed, ends, places),
        lambda: by_groups(embeddings, owner, local_cluster),
    )


def solution(mesh):
    fine = Mesh(mesh.devices.reshape(4, 4, 2, 4), ALL)
    return jax.shard_map(
        body,
        mesh=fine,
        in_specs=(P(ALL, None), P(ALL, None), P(ALL)),
        out_specs=P(ALL),
        check_vma=False,
    )
```

```python
import itertools
import math

import jax
import jax.numpy as jnp
from jax import lax
from jax.experimental import pallas as pl
from jax.experimental.pallas import tpu as pltpu
from jax.sharding import Mesh, PartitionSpec as P

CPG = 16
GROUPS = 32
CLUSTERS = GROUPS * CPG
ROWS = 768
WIDTH = 1024
CHIPS = 64
DEVS = 128
CAP = 24
SLOTS = CHIPS * CAP
TILE = 384
HELD = 896
ALL = ("z", "y", "core", "x")
GROUP_AXES = ("z", "y", "core")
CHIP_AXES = ("z", "y", "x")
ORDERS = tuple(itertools.permutations(range(4)))
BF16 = jnp.bfloat16
ANY = pl.BlockSpec(memory_space=pl.ANY)
HBM = pl.BlockSpec(memory_space=pltpu.HBM)
F32 = jnp.float32


def iota(shape, dim):
    return lax.broadcasted_iota(jnp.int32, shape, dim)


def dot(a, b, ca=1, cb=0, precision=None):
    return lax.dot_general(
        a, b, (((ca,), (cb,)), ((), ())), preferred_element_type=F32, precision=precision
    )


def onehot(cond):
    return jnp.where(cond, 1.0, 0.0).astype(BF16)


def place():
    zy = lax.axis_index("z") * 4 + lax.axis_index("y")
    return lax.axis_index("core"), zy * 4 + lax.axis_index("x")


def count_kernel(owner_ref, local_ref, hist_ref, ids_ref, hists, sem):
    owner = owner_ref[...]
    local = jnp.concatenate([local_ref[j : j + 1, :] for j in range(ROWS // 128)], axis=1)
    by_owner = onehot(owner == iota((GROUPS, ROWS), 0))
    by_local = onehot(local == iota((CPG, ROWS), 0))
    pairs = dot(by_owner, by_local, 1, 1).astype(BF16)
    spread = onehot(iota((CPG, CLUSTERS), 1) % CPG == iota((CPG, CLUSTERS), 0))
    wide = dot(pairs, spread)
    mine = iota((GROUPS, CLUSTERS), 1) // CPG == iota((GROUPS, CLUSTERS), 0)
    counts = jnp.sum(jnp.where(mine, wide, 0.0), axis=0, keepdims=True)
    for j in range(CLUSTERS // 128):
        part = counts[:, j * 128 : (j + 1) * 128]
        hists[:, j, :] = jnp.broadcast_to(part, (DEVS, 128))
    leave = pltpu.make_async_copy(hists, hist_ref, sem)
    leave.start()
    cluster = owner * CPG + local
    eye = iota((128, 128), 0) == iota((128, 128), 1)
    rank = jnp.zeros((1, ROWS), jnp.int32)
    for j in range(ROWS // 128):
        part = jnp.broadcast_to(cluster[:, j * 128 : (j + 1) * 128], (128, 128))
        column = jnp.sum(jnp.where(eye, part, 0), axis=1, keepdims=True)
        width = ROWS - j * 128
        later = iota((128, width), 1) > iota((128, width), 0)
        hit = jnp.where((column == cluster[:, j * 128 :]) & later, 1, 0)
        found = jnp.sum(hit, axis=0, keepdims=True)
        if j:
            found = jnp.concatenate([jnp.zeros((1, j * 128), jnp.int32), found], axis=1)
        rank = rank + found
    which = iota((8, ROWS), 0)
    ids_ref[...] = jnp.where(which == 0, cluster, jnp.where(which == 1, rank, 0))
    leave.wait()


def wide_row(row):
    return jnp.broadcast_to(row.astype(F32), (8, row.shape[1])).astype(BF16)


def parity(cluster):
    return cluster & 1


def before(flags):
    tri = onehot(iota((256, 256), 0) < iota((256, 256), 1))
    seen, parts = jnp.zeros((1, 1), F32), []
    for j in range(ROWS // 256):
        part = flags[:, j * 256 : (j + 1) * 256]
        parts.append(dot(wide_row(part), tri)[0:1] + seen)
        seen = seen + jnp.sum(part, axis=1, keepdims=True)
    return jnp.concatenate(parts, axis=1), seen


def gather_kernel(ids_ref, ids2_ref, emb_ref, emb2_ref, out_ref, ids_out_ref, raw, raw2, sems):
    core, _ = place()
    reads = [
        pltpu.make_async_copy(emb_ref, raw, sems.at[0]),
        pltpu.make_async_copy(emb2_ref, raw2, sems.at[1]),
    ]
    for read in reads:
        read.start()
    ids, ids2 = ids_ref[...], ids2_ref[...]
    flags, flags2 = (jnp.where(parity(i[0:1]) == core, 1.0, 0.0) for i in (ids, ids2))
    slot, total = before(flags)
    slot2, _ = before(flags2)
    slot = jnp.where(flags > 0, slot, -1.0)
    slot2 = jnp.where(flags2 > 0, slot2 + total, -1.0)
    tile = 256
    at = iota((tile, ROWS), 0).astype(F32).astype(BF16)
    owner_of = [
        jnp.concatenate(
            [(i[0:1] >> 4).astype(F32), (i[0:1] & 15).astype(F32), i[1:2].astype(F32), jnp.full((1, ROWS), 1.0 + n)]
            + [jnp.zeros((4, ROWS), F32)],
            axis=0,
        ).astype(BF16)
        for n, i in enumerate((ids, ids2))
    ]
    for read in reads:
        read.wait()
    for low in range(0, HELD, tile):
        high = min(low + tile, HELD)
        picks = [
            jnp.where(jnp.clip(s - low, -1, tile).astype(BF16) == at[: high - low], BF16(1), BF16(0))
            for s in (slot, slot2)
        ]
        out_ref[low:high, :] = (dot(picks[0], raw[...]) + dot(picks[1], raw2[...])).astype(BF16)
        ids_out_ref[:, low:high] = (
            dot(owner_of[0], picks[0], 1, 1) + dot(owner_of[1], picks[1], 1, 1)
        ).astype(jnp.int32)


def rotate(value, by, run=16):
    if by == 0:
        return value
    inside = (iota(value.shape, 1) & (run - 1)) >= by
    return jnp.where(inside, pltpu.roll(value, by, 1), pltpu.roll(value, by + 128 - run, 1))


def settle(base, parts):
    turned = [[rotate(part, r, 4) for r in range(4)] for part in parts]
    tops = [
        jnp.concatenate([jnp.max(base + t[r], axis=0, keepdims=True) for t in turned], axis=0)
        for r in range(4)
    ]
    lane4 = iota(tops[0].shape, 1) & 3
    best = turn = None
    for order in ORDERS:
        turns = [(j - order[j]) & 3 for j in range(4)]
        load, spin = tops[turns[3]], jnp.full(tops[0].shape, turns[3], jnp.int32)
        for j in range(3):
            load = jnp.where(lane4 == j, tops[turns[j]], load)
            spin = jnp.where(lane4 == j, turns[j], spin)
        load = jnp.maximum(load, rotate(load, 1, 4))
        load = jnp.maximum(load, rotate(load, 2, 4))
        if best is None:
            best, turn = load, spin
        else:
            turn = jnp.where(load < best, spin, turn)
            best = jnp.minimum(load, best)
    return best, turn, turned


def placing(parts):
    lane = iota((1, 128), 1)
    base, sources = parts[0], [lane]
    for part in parts[1:3]:
        _, turn, (turned,) = settle(base, [part])
        chosen = turned[0]
        for r in range(1, 4):
            chosen = jnp.where(turn == r, turned[r], chosen)
        base = base + chosen
        sources.append((lane & ~3) | ((lane - turn) & 3))
    loads, turns, _ = settle(base, [rotate(parts[3], 2 * c, 8) for c in range(4)])
    loads = jnp.maximum(loads, rotate(loads, 4, 8))
    best, turn, by = loads[0:1], turns[0:1], jnp.zeros((1, 128), jnp.int32)
    for c in range(1, 4):
        better = loads[c : c + 1] < best
        best = jnp.where(better, loads[c : c + 1], best)
        turn = jnp.where(better, turns[c : c + 1], turn)
        by = jnp.where(better, 2 * c, by)
    run = (lane & ~3) | ((lane - turn) & 3)
    sources.append((lane & ~7) | ((run - by) & 7))
    return jnp.max(best, axis=1, keepdims=True), sources


def column(weights, rows):
    rows = [row.astype(F32) for row in rows]
    rows = jnp.concatenate(rows + [jnp.zeros((8 - len(rows), rows[0].shape[1]), F32)], axis=0)
    which = iota((8, 128), 0)
    weight = jnp.zeros((8, 128), F32)
    for n, w in enumerate(weights):
        weight = jnp.where(which == n, float(w), weight)
    return dot(rows.astype(BF16), weight.astype(BF16), 0, 0)


def same(col, row):
    parts = [onehot(col == row[:, j * 128 : (j + 1) * 128]) for j in range(row.shape[1] // 128)]
    return jnp.concatenate(parts, axis=1)


def place_kernel(
    hist_ref, ids_ref, held_ref, raw_ref, out_ref, ends_ref, rows_ref, load_ref
):
    core, chip = place()
    hist = jnp.concatenate([hist_ref[:, j, :] for j in range(4)], axis=1).astype(BF16)
    dev = iota((CHIPS, DEVS), 1)
    first = (iota((CHIPS, DEVS), 0) >> 2) * 8 + (iota((CHIPS, DEVS), 0) & 3)
    count0 = dot(onehot(dev == first), hist)
    count1 = dot(onehot(dev == first + 4), hist)
    both = (count0 + count1).astype(BF16)

    in_group = onehot((iota((GROUPS, CLUSTERS), 1) >> 4) == iota((GROUPS, CLUSTERS), 0))
    size_row = jnp.sum(dot(both, in_group, 1, 1), axis=0, keepdims=True)
    size_col = jnp.sum(dot(in_group, both, 1, 1), axis=1, keepdims=True)
    lower = iota((GROUPS, GROUPS), 0) < iota((GROUPS, GROUPS), 1)
    ahead = (size_col > size_row) | ((size_col == size_row) & lower)
    order = jnp.sum(jnp.where(ahead, 1.0, 0.0), axis=0, keepdims=True)
    order = dot(wide_row(order), in_group)[0:1].astype(jnp.int32)
    quarter = jnp.where(order < 16, order >> 3, 3 - (order & 1))
    octet = jnp.where(order < 8, order, jnp.where(order < 16, 15 - order, (31 - order) >> 1))
    local = iota((1, CLUSTERS), 1) & 15
    where = column((128, 16, 8, 1), (quarter, octet, local & 1, local >> 1))

    wide = dot(both, same(where, iota((1, CLUSTERS), 1).astype(F32)))
    load, sources = placing([wide[:, p * 128 : (p + 1) * 128] for p in range(4)])
    odd = onehot(parity(iota((CLUSTERS, 128), 0)) == 1)
    of_odd = dot(both, odd)
    of_all = jnp.sum(both.astype(F32), axis=1, keepdims=True)
    held = jnp.max(jnp.maximum(of_odd, of_all - of_odd), axis=0, keepdims=True)[:, 0:1]
    load_ref[...] = jnp.where(held <= HELD, load, 2.0 * CAP).astype(jnp.int32)
    sources = [source + p * 128 for p, source in enumerate(sources)]
    spread = same(where, jnp.concatenate(sources, axis=1).astype(F32))
    count0 = dot(count0.astype(BF16), spread)
    count1 = dot(count1.astype(BF16), spread)

    at = iota((CLUSTERS, 8), 0)
    upto = iota((CLUSTERS, 8), 1)
    mine = (at & 127) == (chip >> 3) * 16 + core * 8 + (chip & 7)
    ends_ref[...] = dot(
        count0.astype(BF16), onehot(mine & ((at >> 7) * 2 <= upto))
    ) + dot(count1.astype(BF16), onehot(mine & ((at >> 7) * 2 + 1 <= upto)))

    here = iota((CHIPS, CLUSTERS), 0) == chip
    own0 = jnp.sum(jnp.where(here, count0, 0.0), axis=0, keepdims=True)
    own1 = jnp.sum(jnp.where(here, count1, 0.0), axis=0, keepdims=True)
    own = own0 + own1
    start = [jnp.zeros((1, 128), F32)]
    for p in range(3):
        start.append(start[-1] + own[:, p * 128 : (p + 1) * 128])
    start0 = jnp.concatenate(start, axis=1)
    start1 = start0 + own0
    device_row = (iota((1, CLUSTERS), 1) & 127).astype(F32)
    by_group = dot(in_group, spread)
    by_local = onehot((iota((CPG, CLUSTERS), 1) & 15) == iota((CPG, CLUSTERS), 0))
    by_local = dot(by_local, spread).astype(BF16)

    def table(row):
        return dot(by_local, (by_group * row).astype(BF16), 1, 1).astype(BF16)

    to_table, table0, table1 = table(device_row), table(start0), table(start1)

    def slots(group, local, rank, start, rows):
        group = onehot(group == iota((GROUPS, rows), 0))
        local = local == iota((CPG, rows), 0)

        def look(table):
            return jnp.sum(jnp.where(local, dot(table, group), 0.0), axis=0, keepdims=True).astype(jnp.int32)

        return look(to_table), look(start) + rank

    ids = ids_ref[...]
    first = jnp.where(core == 0, table0, table1)
    to, k = slots(ids[0:1] >> 4, ids[0:1] & 15, ids[1:2], first, ROWS)
    rows_ref[...] = jnp.concatenate([to, k, jnp.zeros((6, ROWS), jnp.int32)], axis=0)
    held = held_ref[...]
    group, local, rank, whose = (held[n : n + 1] for n in range(4))
    to, k = slots(group, local, rank, first, HELD)
    _, k2 = slots(group, local, rank, jnp.where(core == 0, table1, table0), HELD)
    k = jnp.where(whose == 1, k, k2)
    slot = jnp.where(whose > 0, ((to >> 4) * 8 + (to & 7)) * CAP + k, -1)
    tile = 256
    at = iota((tile, HELD), 0).astype(F32).astype(BF16)
    for n in range(SLOTS // tile):
        pick = jnp.clip(slot - n * tile, -1, tile).astype(F32).astype(BF16)
        rows = dot(jnp.where(pick == at, BF16(1), BF16(0)), raw_ref[...])
        scale = lax.rsqrt(jnp.mean(rows * rows, axis=1, keepdims=True) + 1e-06) / math.sqrt(WIDTH)
        out_ref[n * tile : (n + 1) * tile, :] = (rows * scale).astype(BF16)


def pairs_kernel(rows_ref, ends_ref, out_ref):
    at = iota((1, SLOTS), 1)
    chip = at * 2731 >> 16
    k = at - chip * CAP
    own_chip = chip == iota((CHIPS, SLOTS), 0)
    ends = dot(ends_ref[...].astype(BF16), onehot(own_chip), 0, 0)
    past = jnp.sum(jnp.where(k.astype(F32) >= ends, 1, 0), axis=0, keepdims=True)
    label = past >> 1
    dev = (chip >> 2) * 8 + (past & 1) * 4 + (chip & 3)
    label_col = column((1,), (label,))
    order_col = column((32, 1), (dev, k))
    label_row = label.astype(F32)
    order_row = (dev * 32 + k).astype(F32)
    best = []
    for i in range(SLOTS // TILE):
        mine = slice(i * TILE, (i + 1) * TILE)
        top = jnp.full((1, TILE), -1.0, F32)
        for j in range(i + 1):
            other = slice(j * TILE, (j + 1) * TILE)
            score = dot(rows_ref[other, :], rows_ref[mine, :], 1, 1)
            tops = []
            for c in range(TILE // 128):
                part = slice(i * TILE + c * 128, i * TILE + (c + 1) * 128)
                keep = label_col[other] == label_row[:, part]
                if i == j:
                    keep = keep & (order_col[other] < order_row[:, part])
                part = jnp.where(keep, score[:, c * 128 : (c + 1) * 128], -1.0)
                tops.append(jnp.max(part, axis=0, keepdims=True))
            top = jnp.maximum(top, jnp.concatenate(tops, axis=1))
        best.append(top)
    best = jnp.concatenate(best, axis=1)
    block = jnp.where(own_chip, best, 0.0)
    at = iota((SLOTS, 128), 0)
    place_col = jnp.where(at - (at * 2731 >> 16) * CAP == iota((SLOTS, 128), 1), 1.0, 0.0)
    found = dot(block, place_col, precision=lax.Precision.HIGHEST)
    for n in range(DEVS // 8):
        four = found[n * 4 : (n + 1) * 4, :]
        out_ref[n * 8 : (n + 1) * 8, :] = jnp.concatenate([four, four], axis=0)


def home_kernel(got_ref, rows_ref, out_ref):
    to, k = rows_ref[0:1, :], rows_ref[1:2, :]
    chip = (to >> 4) * 8 + (to & 7)
    dev = (chip >> 2) * 8 + ((to >> 3) & 1) * 4 + (chip & 3)
    pick = jnp.where(dev == iota((DEVS, ROWS), 0), 1.0, 0.0)
    cand = dot(got_ref[:, 0:32], pick, 0, 0, precision=lax.Precision.HIGHEST)
    best = jnp.sum(jnp.where(k == iota((32, ROWS), 0), cand, 0.0), axis=0, keepdims=True)
    for j in range(ROWS // 128):
        out_ref[j : j + 1, :] = best[:, j * 128 : (j + 1) * 128]


def call(kernel, out_shape, *args, vmem=32 * 2**20, **kwargs):
    return pl.pallas_call(
        kernel,
        out_shape=out_shape,
        compiler_params=pltpu.CompilerParams(vmem_limit_bytes=vmem),
        **kwargs,
    )(*args)


def shape(*dims, dtype=F32):
    return jax.ShapeDtypeStruct(dims, dtype)


def by_groups(embeddings, owner, local_cluster):
    rows, width = embeddings.shape
    n_groups = GROUPS
    cap = 2 * rows // n_groups
    emb32 = embeddings.astype(F32)
    scale = lax.rsqrt(jnp.mean(emb32 * emb32, axis=1, keepdims=True) + 1e-06) / math.sqrt(width)
    unit = (emb32 * scale).astype(BF16)
    target = owner[:, 0]
    cluster = target * CPG + local_cluster
    device = lax.axis_index(ALL)
    global_id = device * rows + jnp.arange(rows, dtype=jnp.int32)
    onehots = (target[:, None] == jnp.arange(n_groups, dtype=jnp.int32)[None, :]).astype(jnp.int32)
    rank = jnp.sum(jnp.cumsum(onehots, axis=0) * onehots, axis=1) - 1
    slot = target * cap + rank
    size = n_groups * cap

    def send(x, fill):
        full = jnp.full((size,) + x.shape[1:], fill, x.dtype).at[slot].set(x)
        full = full.reshape((n_groups, cap) + x.shape[1:])
        got = lax.all_to_all(full, GROUP_AXES, split_axis=0, concat_axis=0, tiled=True)
        return got.reshape((size,) + x.shape[1:])

    mine, ids, labels = send(unit, 0), send(global_id, -1), send(cluster, -1)
    rows4, ids4, labels4 = (lax.all_gather(x, "x", axis=0, tiled=True) for x in (mine, ids, labels))
    prod = jnp.einsum("id,jd->ij", mine, rows4, preferred_element_type=F32)
    keep = (labels[:, None] == labels4[None, :]) & (ids4[None, :] < ids[:, None])
    best = jnp.maximum(-1.0, jnp.max(jnp.where(keep, prod, -1.0), axis=1))
    back = lax.all_to_all(
        best.reshape(n_groups, cap), GROUP_AXES, split_axis=0, concat_axis=0, tiled=True
    )
    return back.reshape(size)[slot]


def by_devices(packed, ends):
    blocks = packed.reshape(CHIPS, CAP, WIDTH)
    got = lax.all_to_all(blocks, CHIP_AXES, split_axis=0, concat_axis=0, tiled=True)
    best = call(
        pairs_kernel, shape(DEVS, 128), got.reshape(SLOTS, WIDTH), ends
    )
    return best


def body(embeddings, owner, local_cluster):
    hist, ids = call(
        count_kernel,
        (shape(DEVS, 4, 128), shape(8, ROWS, dtype=jnp.int32)),
        owner.reshape(1, ROWS),
        local_cluster.reshape(ROWS // 128, 128),
        out_specs=(HBM, pl.BlockSpec()),
        scratch_shapes=[pltpu.VMEM((DEVS, 4, 128), F32), pltpu.SemaphoreType.DMA],
    )
    swap = [(0, 1), (1, 0)]
    ids2 = lax.ppermute(ids, "core", swap)
    hists = lax.all_to_all(hist, ALL, split_axis=0, concat_axis=0, tiled=True)
    embeddings2 = lax.ppermute(embeddings, "core", swap)
    raw, held = call(
        gather_kernel,
        (shape(HELD, WIDTH, dtype=BF16), shape(8, HELD, dtype=jnp.int32)),
        ids, ids2, embeddings, embeddings2,
        in_specs=[pl.BlockSpec()] * 2 + [ANY] * 2,
        scratch_shapes=[
            pltpu.VMEM((ROWS, WIDTH), BF16),
            pltpu.VMEM((ROWS, WIDTH), BF16),
            pltpu.SemaphoreType.DMA((2,)),
        ],
    )
    packed, ends, places, load = call(
        place_kernel,
        (
            shape(SLOTS, WIDTH, dtype=BF16),
            shape(CHIPS, 8),
            shape(8, ROWS, dtype=jnp.int32),
            shape(1, 1, dtype=jnp.int32),
        ),
        hists, ids, held, raw,
    )
    best = by_devices(packed, ends)
    back = lax.all_to_all(best, ALL, split_axis=0, concat_axis=0, tiled=True)
    return lax.cond(
        load.reshape(()) <= CAP,
        lambda: call(home_kernel, shape(ROWS // 128, 128), back, places).reshape(ROWS),
        lambda: by_groups(embeddings, owner, local_cluster),
    )


def solution(mesh):
    fine = Mesh(mesh.devices.reshape(4, 4, 2, 4), ALL)
    return jax.shard_map(
        body,
        mesh=fine,
        in_specs=(P(ALL, None), P(ALL, None), P(ALL)),
        out_specs=P(ALL),
        check_vma=False,
    )
```

```python
import itertools
import math

import jax
import jax.numpy as jnp
from jax import lax
from jax.experimental import pallas as pl
from jax.experimental.pallas import tpu as pltpu
from jax.sharding import Mesh, PartitionSpec as P

CPG = 16
GROUPS = 32
CLUSTERS = GROUPS * CPG
ROWS = 768
WIDTH = 1024
CHIPS = 64
DEVS = 128
CAP = 24
SLOTS = CHIPS * CAP
LINE = 4 * CAP
PIECE = 128
ALL = ("z", "y", "core", "x")
GROUP_AXES = ("z", "y", "core")
CHIP_AXES = ("z", "y", "x")
ORDERS = tuple(itertools.permutations(range(4)))
BF16 = jnp.bfloat16
ANY = pl.BlockSpec(memory_space=pl.ANY)
HBM = pl.BlockSpec(memory_space=pltpu.HBM)
F32 = jnp.float32


def iota(shape, dim):
    return lax.broadcasted_iota(jnp.int32, shape, dim)


def dot(a, b, ca=1, cb=0):
    return lax.dot_general(a, b, (((ca,), (cb,)), ((), ())), preferred_element_type=F32)


def onehot(cond):
    return jnp.where(cond, 1.0, 0.0).astype(BF16)


def place():
    zy = lax.axis_index("z") * 4 + lax.axis_index("y")
    return lax.axis_index("core"), zy * 4 + lax.axis_index("x")


def count_kernel(owner_ref, local_ref, hist_ref, ids_ref, hists, sem):
    owner = owner_ref[...]
    local = jnp.concatenate([local_ref[j : j + 1, :] for j in range(ROWS // 128)], axis=1)
    by_owner = onehot(owner == iota((GROUPS, ROWS), 0))
    by_local = onehot(local == iota((CPG, ROWS), 0))
    pairs = dot(by_owner, by_local, 1, 1).astype(BF16)
    spread = onehot(iota((CPG, CLUSTERS), 1) % CPG == iota((CPG, CLUSTERS), 0))
    wide = dot(pairs, spread)
    mine = iota((GROUPS, CLUSTERS), 1) // CPG == iota((GROUPS, CLUSTERS), 0)
    counts = jnp.sum(jnp.where(mine, wide, 0.0), axis=0, keepdims=True)
    for j in range(CLUSTERS // 128):
        part = counts[:, j * 128 : (j + 1) * 128]
        hists[:, j, :] = jnp.broadcast_to(part, (DEVS, 128))
    leave = pltpu.make_async_copy(hists, hist_ref, sem)
    leave.start()
    cluster = owner * CPG + local
    eye = iota((128, 128), 0) == iota((128, 128), 1)
    rank = jnp.zeros((1, ROWS), jnp.int32)
    for j in range(ROWS // 128):
        part = jnp.broadcast_to(cluster[:, j * 128 : (j + 1) * 128], (128, 128))
        column = jnp.sum(jnp.where(eye, part, 0), axis=1, keepdims=True)
        width = ROWS - j * 128
        later = iota((128, width), 1) > iota((128, width), 0)
        hit = jnp.where((column == cluster[:, j * 128 :]) & later, 1, 0)
        found = jnp.sum(hit, axis=0, keepdims=True)
        if j:
            found = jnp.concatenate([jnp.zeros((1, j * 128), jnp.int32), found], axis=1)
        rank = rank + found
    which = iota((8, ROWS), 0)
    ids_ref[...] = jnp.where(which == 0, cluster, jnp.where(which == 1, rank, 0))
    leave.wait()


def wide_row(row):
    return jnp.broadcast_to(row.astype(F32), (8, row.shape[1])).astype(BF16)


def parity(cluster):
    return cluster & 1


def rotate(value, by, run=16):
    if by == 0:
        return value
    inside = (iota(value.shape, 1) & (run - 1)) >= by
    return jnp.where(inside, pltpu.roll(value, by, 1), pltpu.roll(value, by + 128 - run, 1))


def settle(base, parts):
    turned = [[rotate(part, r, 4) for r in range(4)] for part in parts]
    tops = [
        jnp.concatenate([jnp.max(base + t[r], axis=0, keepdims=True) for t in turned], axis=0)
        for r in range(4)
    ]
    lane4 = iota(tops[0].shape, 1) & 3
    best = turn = None
    for order in ORDERS:
        turns = [(j - order[j]) & 3 for j in range(4)]
        load, spin = tops[turns[3]], jnp.full(tops[0].shape, turns[3], jnp.int32)
        for j in range(3):
            load = jnp.where(lane4 == j, tops[turns[j]], load)
            spin = jnp.where(lane4 == j, turns[j], spin)
        load = jnp.maximum(load, rotate(load, 1, 4))
        load = jnp.maximum(load, rotate(load, 2, 4))
        if best is None:
            best, turn = load, spin
        else:
            turn = jnp.where(load < best, spin, turn)
            best = jnp.minimum(load, best)
    return best, turn, turned


def placing(parts, carried):
    base, placed = parts[0], [carried[0]]
    for part, rows in zip(parts[1:3], carried[1:3]):
        _, turn, (turned,) = settle(base, [part])
        base = base + spun(turned, turn)
        placed.append(spun([rotate(rows, r, 4) for r in range(4)], turn))
    loads, turns, _ = settle(base, [rotate(parts[3], 2 * c, 8) for c in range(4)])
    loads = jnp.maximum(loads, rotate(loads, 4, 8))
    best, turn, by = loads[0:1], turns[0:1], jnp.zeros((1, 128), jnp.int32)
    for c in range(1, 4):
        better = loads[c : c + 1] < best
        best = jnp.where(better, loads[c : c + 1], best)
        turn = jnp.where(better, turns[c : c + 1], turn)
        by = jnp.where(better, c, by)
    rows = spun([rotate(carried[3], 2 * c, 8) for c in range(4)], by)
    placed.append(spun([rotate(rows, r, 4) for r in range(4)], turn))
    return jnp.max(best, axis=1, keepdims=True), placed


def spun(turned, turn):
    rows = turned[0]
    for r in range(1, 4):
        rows = jnp.where(turn == r, turned[r], rows)
    return rows


def column(weights, rows):
    rows = [row.astype(F32) for row in rows]
    rows = jnp.concatenate(rows + [jnp.zeros((8 - len(rows), rows[0].shape[1]), F32)], axis=0)
    which = iota((8, 128), 0)
    weight = jnp.zeros((8, 128), F32)
    for n, w in enumerate(weights):
        weight = jnp.where(which == n, float(w), weight)
    return dot(rows.astype(BF16), weight.astype(BF16), 0, 0)


def same(col, row):
    parts = [onehot(col == row[:, j * 128 : (j + 1) * 128]) for j in range(row.shape[1] // 128)]
    return jnp.concatenate(parts, axis=1)


def place_kernel(
    hist_ref, ids_ref, ids2_ref, emb_ref, emb2_ref, out_ref, ends_ref, rows_ref, load_ref, raw, sems
):
    core, chip = place()
    reads = [
        pltpu.make_async_copy(
            source.at[pl.ds(n * PIECE, PIECE), :],
            raw.at[pl.ds(i * ROWS + n * PIECE, PIECE), :],
            sems.at[i, n],
        )
        for n in range(ROWS // PIECE)
        for i, source in enumerate((emb_ref, emb2_ref))
    ]
    for read in reads:
        read.start()
    hist = jnp.concatenate([hist_ref[:, j, :] for j in range(4)], axis=1).astype(BF16)
    dev = iota((CHIPS, DEVS), 1)
    first = (iota((CHIPS, DEVS), 0) >> 2) * 8 + (iota((CHIPS, DEVS), 0) & 3)
    count0 = dot(onehot(dev == first), hist)
    count1 = dot(onehot(dev == first + 4), hist)
    both = (count0 + count1).astype(BF16)

    in_group = onehot((iota((GROUPS, CLUSTERS), 1) >> 4) == iota((GROUPS, CLUSTERS), 0))
    size_row = jnp.sum(dot(both, in_group, 1, 1), axis=0, keepdims=True)
    size_col = jnp.sum(dot(in_group, both, 1, 1), axis=1, keepdims=True)
    lower = iota((GROUPS, GROUPS), 0) < iota((GROUPS, GROUPS), 1)
    ahead = (size_col > size_row) | ((size_col == size_row) & lower)
    order = jnp.sum(jnp.where(ahead, 1.0, 0.0), axis=0, keepdims=True)
    order = dot(wide_row(order), in_group)[0:1].astype(jnp.int32)
    quarter = jnp.where(order < 16, order >> 3, 3 - (order & 1))
    octet = jnp.where(order < 8, order, jnp.where(order < 16, 15 - order, (31 - order) >> 1))
    local = iota((1, CLUSTERS), 1) & 15
    where = column((128, 16, 8, 1), (quarter, octet, local & 1, local >> 1))

    spread = same(where, iota((1, CLUSTERS), 1).astype(F32))
    names = (iota((8, CLUSTERS), 1) >> 4, iota((8, CLUSTERS), 1) & 15)
    names = jnp.where(iota((8, CLUSTERS), 0) == 0, *names).astype(F32)
    wide = dot(jnp.concatenate([count0, count1, names], axis=0).astype(BF16), spread)
    quarters = [wide[:, p * 128 : (p + 1) * 128] for p in range(4)]
    load, placed = placing([w[:CHIPS] + w[CHIPS:DEVS] for w in quarters], quarters)
    load_ref[...] = load.astype(jnp.int32)
    placed = jnp.concatenate(placed, axis=1)
    count0, count1, names = placed[:CHIPS], placed[CHIPS:DEVS], placed[DEVS:].astype(jnp.int32)
    at = iota((CLUSTERS, 8), 0)
    upto = iota((CLUSTERS, 8), 1)
    mine = (at & 127) == (chip >> 3) * 16 + core * 8 + (chip & 7)
    ends_ref[...] = dot(
        count0.astype(BF16), onehot(mine & ((at >> 7) * 2 <= upto))
    ) + dot(count1.astype(BF16), onehot(mine & ((at >> 7) * 2 + 1 <= upto)))

    here = iota((CHIPS, CLUSTERS), 0) == chip
    own0 = jnp.sum(jnp.where(here, count0, 0.0), axis=0, keepdims=True)
    own1 = jnp.sum(jnp.where(here, count1, 0.0), axis=0, keepdims=True)
    own = own0 + own1
    start = [jnp.zeros((1, 128), F32)]
    for p in range(3):
        start.append(start[-1] + own[:, p * 128 : (p + 1) * 128])
    start0 = jnp.concatenate(start, axis=1)
    start1 = start0 + own0
    device_row = (iota((1, CLUSTERS), 1) & 127).astype(F32)
    by_group = jnp.where(names[0:1] == iota((GROUPS, CLUSTERS), 0), 1.0, 0.0)
    by_local = onehot(names[1:2] == iota((CPG, CLUSTERS), 0))

    def table(row):
        return dot(by_local, (by_group * row).astype(BF16), 1, 1).astype(BF16)

    to_table, table0, table1 = table(device_row), table(start0), table(start1)

    def slots(ids, start):
        group = onehot((ids[0:1] >> 4) == iota((GROUPS, ROWS), 0))
        local = (ids[0:1] & 15) == iota((CPG, ROWS), 0)

        def look(table):
            return jnp.sum(jnp.where(local, dot(table, group), 0.0), axis=0, keepdims=True).astype(jnp.int32)

        to = look(to_table)
        k = look(start) + ids[1:2]
        return to, k, jnp.where(((to >> 3) & 1) == core, ((to >> 4) * 8 + (to & 7)) * CAP + k, -1)

    to, k, slot = slots(ids_ref[...], jnp.where(core == 0, table0, table1))
    _, _, slot2 = slots(ids2_ref[...], jnp.where(core == 0, table1, table0))
    rows_ref[...] = jnp.concatenate([to, k, jnp.zeros((6, ROWS), jnp.int32)], axis=0)
    slot = jnp.concatenate([slot, slot2], axis=1)
    for read in reads:
        read.wait()
    tile = 256
    at = iota((tile, 2 * ROWS), 0).astype(F32).astype(BF16)
    for n in range(SLOTS // tile):
        pick = jnp.clip(slot - n * tile, -1, tile).astype(F32).astype(BF16)
        rows = dot(jnp.where(pick == at, BF16(1), BF16(0)), raw[...])
        scale = lax.rsqrt(jnp.mean(rows * rows, axis=1, keepdims=True) + 1e-06) / math.sqrt(WIDTH)
        out_ref[n * tile : (n + 1) * tile, :] = (rows * scale).astype(BF16)


def moved(values, picks, *dims):
    total = None
    for _ in range(3):
        part = values.astype(BF16)
        values = values - part.astype(F32)
        product = dot(part, picks, *dims)
        total = product if total is None else total + product
    return total


def pairs_kernel(rows_ref, ends_ref, out_ref):
    at = iota((1, SLOTS), 1)
    chip = at * 2731 >> 16
    k = at - chip * CAP
    own_chip = chip == iota((CHIPS, SLOTS), 0)
    ends = dot(ends_ref[...].astype(BF16), onehot(own_chip), 0, 0)
    past = jnp.sum(jnp.where(k.astype(F32) >= ends, 1, 0), axis=0, keepdims=True)
    label = past >> 1
    dev = (chip >> 2) * 8 + (past & 1) * 4 + (chip & 3)
    label_col = column((1,), (label,))
    order_col = column((32, 1), (dev, k))
    label_row = label.astype(F32)
    order_row = (dev * 32 + k).astype(F32)
    best = []
    for low in range(0, SLOTS, 256):
        mine = slice(low, low + 256)
        sure, end = low // LINE * LINE, -(-(low + 256) // LINE) * LINE
        top = jnp.full((1, 256), -1.0, F32)
        for first, last in ((0, sure), (sure, end)):
            if first == last:
                continue
            other = slice(first, last)
            score = dot(rows_ref[other, :], rows_ref[mine, :], 1, 1)
            tops = []
            for c in range(2):
                part = slice(low + c * 128, low + (c + 1) * 128)
                keep = label_col[other] == label_row[:, part]
                if first == sure:
                    keep = keep & (order_col[other] < order_row[:, part])
                part = jnp.where(keep, score[:, c * 128 : (c + 1) * 128], -1.0)
                tops.append(jnp.max(part, axis=0, keepdims=True))
            top = jnp.maximum(top, jnp.concatenate(tops, axis=1))
        best.append(top)
    best = jnp.concatenate(best, axis=1)
    block = jnp.where(own_chip, best, 0.0)
    at = iota((SLOTS, 128), 0)
    place_col = at - (at * 2731 >> 16) * CAP == iota((SLOTS, 128), 1)
    found = moved(block, onehot(place_col))
    for n in range(DEVS // 8):
        four = found[n * 4 : (n + 1) * 4, :]
        out_ref[n * 8 : (n + 1) * 8, :] = jnp.concatenate([four, four], axis=0)


def home_kernel(got_ref, rows_ref, out_ref):
    to, k = rows_ref[0:1, :], rows_ref[1:2, :]
    chip = (to >> 4) * 8 + (to & 7)
    dev = (chip >> 2) * 8 + ((to >> 3) & 1) * 4 + (chip & 3)
    cand = moved(got_ref[:, 0:32], onehot(dev == iota((DEVS, ROWS), 0)), 0, 0)
    best = jnp.sum(jnp.where(k == iota((32, ROWS), 0), cand, 0.0), axis=0, keepdims=True)
    for j in range(ROWS // 128):
        out_ref[j : j + 1, :] = best[:, j * 128 : (j + 1) * 128]


def call(kernel, out_shape, *args, vmem=32 * 2**20, **kwargs):
    return pl.pallas_call(
        kernel,
        out_shape=out_shape,
        compiler_params=pltpu.CompilerParams(vmem_limit_bytes=vmem),
        **kwargs,
    )(*args)


def shape(*dims, dtype=F32):
    return jax.ShapeDtypeStruct(dims, dtype)


def by_groups(embeddings, owner, local_cluster):
    rows, width = embeddings.shape
    n_groups = GROUPS
    cap = 2 * rows // n_groups
    emb32 = embeddings.astype(F32)
    scale = lax.rsqrt(jnp.mean(emb32 * emb32, axis=1, keepdims=True) + 1e-06) / math.sqrt(width)
    unit = (emb32 * scale).astype(BF16)
    target = owner[:, 0]
    cluster = target * CPG + local_cluster
    device = lax.axis_index(ALL)
    global_id = device * rows + jnp.arange(rows, dtype=jnp.int32)
    onehots = (target[:, None] == jnp.arange(n_groups, dtype=jnp.int32)[None, :]).astype(jnp.int32)
    rank = jnp.sum(jnp.cumsum(onehots, axis=0) * onehots, axis=1) - 1
    slot = target * cap + rank
    size = n_groups * cap

    def send(x, fill):
        full = jnp.full((size,) + x.shape[1:], fill, x.dtype).at[slot].set(x)
        full = full.reshape((n_groups, cap) + x.shape[1:])
        got = lax.all_to_all(full, GROUP_AXES, split_axis=0, concat_axis=0, tiled=True)
        return got.reshape((size,) + x.shape[1:])

    mine, ids, labels = send(unit, 0), send(global_id, -1), send(cluster, -1)
    rows4, ids4, labels4 = (lax.all_gather(x, "x", axis=0, tiled=True) for x in (mine, ids, labels))
    prod = jnp.einsum("id,jd->ij", mine, rows4, preferred_element_type=F32)
    keep = (labels[:, None] == labels4[None, :]) & (ids4[None, :] < ids[:, None])
    best = jnp.maximum(-1.0, jnp.max(jnp.where(keep, prod, -1.0), axis=1))
    back = lax.all_to_all(
        best.reshape(n_groups, cap), GROUP_AXES, split_axis=0, concat_axis=0, tiled=True
    )
    return back.reshape(size)[slot]


def by_devices(packed, ends):
    blocks = packed.reshape(CHIPS, CAP, WIDTH)
    got = lax.all_to_all(blocks, CHIP_AXES, split_axis=0, concat_axis=0, tiled=True)
    best = call(
        pairs_kernel, shape(DEVS, 128), got.reshape(SLOTS, WIDTH), ends
    )
    return best


def body(embeddings, owner, local_cluster):
    hist, ids = call(
        count_kernel,
        (shape(DEVS, 4, 128), shape(8, ROWS, dtype=jnp.int32)),
        owner.reshape(1, ROWS),
        local_cluster.reshape(ROWS // 128, 128),
        out_specs=(HBM, pl.BlockSpec()),
        scratch_shapes=[pltpu.VMEM((DEVS, 4, 128), F32), pltpu.SemaphoreType.DMA],
    )
    swap = [(0, 1), (1, 0)]
    ids2 = lax.ppermute(ids, "core", swap)
    hists = lax.all_to_all(hist, ALL, split_axis=0, concat_axis=0, tiled=True)
    embeddings2 = lax.ppermute(embeddings, "core", swap)
    packed, ends, places, load = call(
        place_kernel,
        (
            shape(SLOTS, WIDTH, dtype=BF16),
            shape(CHIPS, 8),
            shape(8, ROWS, dtype=jnp.int32),
            shape(1, 1, dtype=jnp.int32),
        ),
        hists, ids, ids2, embeddings, embeddings2,
        in_specs=[pl.BlockSpec()] * 3 + [ANY] * 2,
        scratch_shapes=[
            pltpu.VMEM((2 * ROWS, WIDTH), BF16),
            pltpu.SemaphoreType.DMA((2, ROWS // PIECE)),
        ],
    )
    best = by_devices(packed, ends)
    back = lax.all_to_all(best, ALL, split_axis=0, concat_axis=0, tiled=True)
    return lax.cond(
        load.reshape(()) <= CAP,
        lambda: call(home_kernel, shape(ROWS // 128, 128), back, places).reshape(ROWS),
        lambda: by_groups(embeddings, owner, local_cluster),
    )


def solution(mesh):
    fine = Mesh(mesh.devices.reshape(4, 4, 2, 4), ALL)
    return jax.shard_map(
        body,
        mesh=fine,
        in_specs=(P(ALL, None), P(ALL, None), P(ALL)),
        out_specs=P(ALL),
        check_vma=False,
    )
```

```python
import itertools
import math

import jax
import jax.numpy as jnp
from jax import lax
from jax.experimental import pallas as pl
from jax.experimental.pallas import tpu as pltpu
from jax.sharding import Mesh, PartitionSpec as P

CPG = 16
GROUPS = 32
CLUSTERS = GROUPS * CPG
ROWS = 768
WIDTH = 1024
CHIPS = 64
DEVS = 128
CAP = 24
SLOTS = CHIPS * CAP
LINE = 4 * CAP
PIECE = 128
ALL = ("z", "y", "core", "x")
GROUP_AXES = ("z", "y", "core")
CHIP_AXES = ("z", "y", "x")
ORDERS = tuple(itertools.permutations(range(4)))
BF16 = jnp.bfloat16
ANY = pl.BlockSpec(memory_space=pl.ANY)
HBM = pl.BlockSpec(memory_space=pltpu.HBM)
F32 = jnp.float32


def iota(shape, dim):
    return lax.broadcasted_iota(jnp.int32, shape, dim)


def dot(a, b, ca=1, cb=0):
    return lax.dot_general(a, b, (((ca,), (cb,)), ((), ())), preferred_element_type=F32)


def onehot(cond):
    return jnp.where(cond, 1.0, 0.0).astype(BF16)


def place():
    zy = lax.axis_index("z") * 4 + lax.axis_index("y")
    return lax.axis_index("core"), zy * 4 + lax.axis_index("x")


def count_kernel(owner_ref, local_ref, hist_ref, ids_ref, hists, sem):
    owner = owner_ref[...]
    local = jnp.concatenate([local_ref[j : j + 1, :] for j in range(ROWS // 128)], axis=1)
    by_owner = onehot(owner == iota((GROUPS, ROWS), 0))
    by_local = onehot(local == iota((CPG, ROWS), 0))
    pairs = dot(by_owner, by_local, 1, 1).astype(BF16)
    spread = onehot(iota((CPG, CLUSTERS), 1) % CPG == iota((CPG, CLUSTERS), 0))
    wide = dot(pairs, spread)
    mine = iota((GROUPS, CLUSTERS), 1) // CPG == iota((GROUPS, CLUSTERS), 0)
    counts = jnp.sum(jnp.where(mine, wide, 0.0), axis=0, keepdims=True)
    for j in range(CLUSTERS // 128):
        part = counts[:, j * 128 : (j + 1) * 128]
        hists[:, j, :] = jnp.broadcast_to(part, (DEVS, 128))
    leave = pltpu.make_async_copy(hists, hist_ref, sem)
    leave.start()
    cluster = owner * CPG + local
    eye = iota((128, 128), 0) == iota((128, 128), 1)
    rank = jnp.zeros((1, ROWS), jnp.int32)
    for j in range(ROWS // 128):
        part = jnp.broadcast_to(cluster[:, j * 128 : (j + 1) * 128], (128, 128))
        column = jnp.sum(jnp.where(eye, part, 0), axis=1, keepdims=True)
        width = ROWS - j * 128
        later = iota((128, width), 1) > iota((128, width), 0)
        hit = jnp.where((column == cluster[:, j * 128 :]) & later, 1, 0)
        found = jnp.sum(hit, axis=0, keepdims=True)
        if j:
            found = jnp.concatenate([jnp.zeros((1, j * 128), jnp.int32), found], axis=1)
        rank = rank + found
    which = iota((8, ROWS), 0)
    ids_ref[...] = jnp.where(which == 0, cluster, jnp.where(which == 1, rank, 0))
    leave.wait()


def wide_row(row):
    return jnp.broadcast_to(row.astype(F32), (8, row.shape[1])).astype(BF16)


def parity(cluster):
    return cluster & 1


def rotate(value, by, run=16):
    if by == 0:
        return value
    inside = (iota(value.shape, 1) & (run - 1)) >= by
    return jnp.where(inside, pltpu.roll(value, by, 1), pltpu.roll(value, by + 128 - run, 1))


def settle(base, parts):
    turned = [[rotate(part, r, 4) for r in range(4)] for part in parts]
    tops = [
        jnp.concatenate([jnp.max(base + t[r], axis=0, keepdims=True) for t in turned], axis=0)
        for r in range(4)
    ]
    lane4 = iota(tops[0].shape, 1) & 3
    best = turn = None
    for order in ORDERS:
        turns = [(j - order[j]) & 3 for j in range(4)]
        load, spin = tops[turns[3]], jnp.full(tops[0].shape, turns[3], jnp.int32)
        for j in range(3):
            load = jnp.where(lane4 == j, tops[turns[j]], load)
            spin = jnp.where(lane4 == j, turns[j], spin)
        load = jnp.maximum(load, rotate(load, 1, 4))
        load = jnp.maximum(load, rotate(load, 2, 4))
        if best is None:
            best, turn = load, spin
        else:
            turn = jnp.where(load < best, spin, turn)
            best = jnp.minimum(load, best)
    return best, turn, turned


def placing(parts, carried):
    base, placed = parts[0], [carried[0]]
    for part, rows in zip(parts[1:3], carried[1:3]):
        _, turn, (turned,) = settle(base, [part])
        base = base + spun(turned, turn)
        placed.append(spun([rotate(rows, r, 4) for r in range(4)], turn))
    loads, turns, _ = settle(base, [rotate(parts[3], 2 * c, 8) for c in range(4)])
    loads = jnp.maximum(loads, rotate(loads, 4, 8))
    best, turn, by = loads[0:1], turns[0:1], jnp.zeros((1, 128), jnp.int32)
    for c in range(1, 4):
        better = loads[c : c + 1] < best
        best = jnp.where(better, loads[c : c + 1], best)
        turn = jnp.where(better, turns[c : c + 1], turn)
        by = jnp.where(better, c, by)
    rows = spun([rotate(carried[3], 2 * c, 8) for c in range(4)], by)
    placed.append(spun([rotate(rows, r, 4) for r in range(4)], turn))
    return jnp.max(best, axis=1, keepdims=True), placed


def spun(turned, turn):
    rows = turned[0]
    for r in range(1, 4):
        rows = jnp.where(turn == r, turned[r], rows)
    return rows


def column(weights, rows):
    rows = [row.astype(F32) for row in rows]
    rows = jnp.concatenate(rows + [jnp.zeros((8 - len(rows), rows[0].shape[1]), F32)], axis=0)
    which = iota((8, 128), 0)
    weight = jnp.zeros((8, 128), F32)
    for n, w in enumerate(weights):
        weight = jnp.where(which == n, float(w), weight)
    return dot(rows.astype(BF16), weight.astype(BF16), 0, 0)


def same(col, row):
    parts = [onehot(col == row[:, j * 128 : (j + 1) * 128]) for j in range(row.shape[1] // 128)]
    return jnp.concatenate(parts, axis=1)


def place_kernel(
    hist_ref, ids_ref, ids2_ref, emb_ref, emb2_ref, out_ref, ends_ref, rows_ref, load_ref, raw, sems
):
    core, chip = place()
    reads = [
        pltpu.make_async_copy(
            source.at[pl.ds(n * PIECE, PIECE), :],
            raw.at[pl.ds(i * ROWS + n * PIECE, PIECE), :],
            sems.at[i, n],
        )
        for n in range(ROWS // PIECE)
        for i, source in enumerate((emb_ref, emb2_ref))
    ]
    for read in reads:
        read.start()
    hist = jnp.concatenate([hist_ref[:, j, :] for j in range(4)], axis=1).astype(BF16)
    dev = iota((CHIPS, DEVS), 1)
    first = (iota((CHIPS, DEVS), 0) >> 2) * 8 + (iota((CHIPS, DEVS), 0) & 3)
    count0 = dot(onehot(dev == first), hist)
    count1 = dot(onehot(dev == first + 4), hist)
    both = (count0 + count1).astype(BF16)

    in_group = onehot((iota((GROUPS, CLUSTERS), 1) >> 4) == iota((GROUPS, CLUSTERS), 0))
    size_row = jnp.sum(dot(both, in_group, 1, 1), axis=0, keepdims=True)
    size_col = jnp.sum(dot(in_group, both, 1, 1), axis=1, keepdims=True)
    lower = iota((GROUPS, GROUPS), 0) < iota((GROUPS, GROUPS), 1)
    ahead = (size_col > size_row) | ((size_col == size_row) & lower)
    order = jnp.sum(jnp.where(ahead, 1.0, 0.0), axis=0, keepdims=True)
    order = dot(wide_row(order), in_group)[0:1].astype(jnp.int32)
    quarter = jnp.where(order < 16, order >> 3, 3 - (order & 1))
    octet = jnp.where(order < 8, order, jnp.where(order < 16, 15 - order, (31 - order) >> 1))
    local = iota((1, CLUSTERS), 1) & 15
    where = column((128, 16, 8, 1), (quarter, octet, local & 1, local >> 1))

    spread = same(where, iota((1, CLUSTERS), 1).astype(F32))
    names = (iota((8, CLUSTERS), 1) >> 4, iota((8, CLUSTERS), 1) & 15)
    names = jnp.where(iota((8, CLUSTERS), 0) == 0, *names).astype(F32)
    wide = dot(jnp.concatenate([count0, count1, names], axis=0).astype(BF16), spread)
    quarters = [wide[:, p * 128 : (p + 1) * 128] for p in range(4)]
    load, placed = placing([w[:CHIPS] + w[CHIPS:DEVS] for w in quarters], quarters)
    load_ref[...] = load.astype(jnp.int32)
    placed = jnp.concatenate(placed, axis=1)
    count0, count1, names = placed[:CHIPS], placed[CHIPS:DEVS], placed[DEVS:].astype(jnp.int32)
    at = iota((CLUSTERS, 8), 0)
    upto = iota((CLUSTERS, 8), 1)
    mine = (at & 127) == (chip >> 3) * 16 + core * 8 + (chip & 7)
    ends_ref[...] = dot(
        count0.astype(BF16), onehot(mine & ((at >> 7) * 2 <= upto))
    ) + dot(count1.astype(BF16), onehot(mine & ((at >> 7) * 2 + 1 <= upto)))

    here = iota((CHIPS, CLUSTERS), 0) == chip
    own0 = jnp.sum(jnp.where(here, count0, 0.0), axis=0, keepdims=True)
    own1 = jnp.sum(jnp.where(here, count1, 0.0), axis=0, keepdims=True)
    own = own0 + own1
    start = [jnp.zeros((1, 128), F32)]
    for p in range(3):
        start.append(start[-1] + own[:, p * 128 : (p + 1) * 128])
    start0 = jnp.concatenate(start, axis=1)
    start1 = start0 + own0
    device_row = (iota((1, CLUSTERS), 1) & 127).astype(F32)
    by_group = jnp.where(names[0:1] == iota((GROUPS, CLUSTERS), 0), 1.0, 0.0)
    by_local = onehot(names[1:2] == iota((CPG, CLUSTERS), 0))

    def table(row):
        return dot(by_local, (by_group * row).astype(BF16), 1, 1).astype(BF16)

    to_table, table0, table1 = table(device_row), table(start0), table(start1)

    def slots(ids, start):
        group = onehot((ids[0:1] >> 4) == iota((GROUPS, ROWS), 0))
        local = (ids[0:1] & 15) == iota((CPG, ROWS), 0)

        def look(table):
            return jnp.sum(jnp.where(local, dot(table, group), 0.0), axis=0, keepdims=True).astype(jnp.int32)

        to = look(to_table)
        k = look(start) + ids[1:2]
        return to, k, jnp.where(((to >> 3) & 1) == core, ((to >> 4) * 8 + (to & 7)) * CAP + k, -1)

    to, k, slot = slots(ids_ref[...], jnp.where(core == 0, table0, table1))
    _, _, slot2 = slots(ids2_ref[...], jnp.where(core == 0, table1, table0))
    rows_ref[...] = jnp.concatenate([to, k, jnp.zeros((6, ROWS), jnp.int32)], axis=0)
    slot = jnp.concatenate([slot, slot2], axis=1)
    for read in reads:
        read.wait()
    tile = 256
    at = iota((tile, 2 * ROWS), 0).astype(F32).astype(BF16)
    for n in range(SLOTS // tile):
        pick = jnp.clip(slot - n * tile, -1, tile).astype(F32).astype(BF16)
        rows = dot(jnp.where(pick == at, BF16(1), BF16(0)), raw[...])
        scale = lax.rsqrt(jnp.mean(rows * rows, axis=1, keepdims=True) + 1e-06) / math.sqrt(WIDTH)
        out_ref[n * tile : (n + 1) * tile, :] = (rows * scale).astype(BF16)


def moved(values, picks, *dims):
    total = None
    for _ in range(3):
        part = values.astype(BF16)
        values = values - part.astype(F32)
        product = dot(part, picks, *dims)
        total = product if total is None else total + product
    return total


def pairs_kernel(rows_ref, ends_ref, out_ref):
    at = iota((1, SLOTS), 1)
    chip = at * 2731 >> 16
    k = at - chip * CAP
    own_chip = chip == iota((CHIPS, SLOTS), 0)
    ends = dot(ends_ref[...].astype(BF16), onehot(own_chip), 0, 0)
    past = jnp.sum(jnp.where(k.astype(F32) >= ends, 1, 0), axis=0, keepdims=True)
    label = past >> 1
    dev = (chip >> 2) * 8 + (past & 1) * 4 + (chip & 3)
    label_col = column((1,), (label,))
    order_col = column((32, 1), (dev, k))
    label_row = label.astype(F32)
    order_row = (dev * 32 + k).astype(F32)
    best = []
    for low in range(0, SLOTS, 256):
        mine = slice(low, low + 256)
        sure, end = low // LINE * LINE, -(-(low + 256) // LINE) * LINE
        top = jnp.full((1, 256), -1.0, F32)
        for first, last in ((0, sure), (sure, end)):
            if first == last:
                continue
            other = slice(first, last)
            score = dot(rows_ref[other, :], rows_ref[mine, :], 1, 1)
            tops = []
            for c in range(2):
                part = slice(low + c * 128, low + (c + 1) * 128)
                keep = label_col[other] == label_row[:, part]
                if first == sure:
                    keep = keep & (order_col[other] < order_row[:, part])
                part = jnp.where(keep, score[:, c * 128 : (c + 1) * 128], -1.0)
                tops.append(jnp.max(part, axis=0, keepdims=True))
            top = jnp.maximum(top, jnp.concatenate(tops, axis=1))
        best.append(top)
    best = jnp.concatenate(best, axis=1)
    block = jnp.where(own_chip, best, 0.0)
    at = iota((SLOTS, 128), 0)
    place_col = at - (at * 2731 >> 16) * CAP == iota((SLOTS, 128), 1)
    found = moved(block, onehot(place_col))
    for n in range(DEVS // 8):
        four = found[n * 4 : (n + 1) * 4, :]
        out_ref[n * 8 : (n + 1) * 8, :] = jnp.concatenate([four, four], axis=0)


def home_kernel(got_ref, rows_ref, out_ref):
    to, k = rows_ref[0:1, :], rows_ref[1:2, :]
    chip = (to >> 4) * 8 + (to & 7)
    dev = (chip >> 2) * 8 + ((to >> 3) & 1) * 4 + (chip & 3)
    cand = moved(got_ref[:, 0:32], onehot(dev == iota((DEVS, ROWS), 0)), 0, 0)
    best = jnp.sum(jnp.where(k == iota((32, ROWS), 0), cand, 0.0), axis=0, keepdims=True)
    for j in range(ROWS // 128):
        out_ref[j : j + 1, :] = best[:, j * 128 : (j + 1) * 128]


def call(kernel, out_shape, *args, vmem=32 * 2**20, **kwargs):
    return pl.pallas_call(
        kernel,
        out_shape=out_shape,
        compiler_params=pltpu.CompilerParams(vmem_limit_bytes=vmem),
        **kwargs,
    )(*args)


def shape(*dims, dtype=F32):
    return jax.ShapeDtypeStruct(dims, dtype)


def by_groups(embeddings, owner, local_cluster):
    rows, width = embeddings.shape
    n_groups = GROUPS
    cap = 2 * rows // n_groups
    emb32 = embeddings.astype(F32)
    scale = lax.rsqrt(jnp.mean(emb32 * emb32, axis=1, keepdims=True) + 1e-06) / math.sqrt(width)
    unit = (emb32 * scale).astype(BF16)
    target = owner[:, 0]
    cluster = target * CPG + local_cluster
    device = lax.axis_index(ALL)
    global_id = device * rows + jnp.arange(rows, dtype=jnp.int32)
    onehots = (target[:, None] == jnp.arange(n_groups, dtype=jnp.int32)[None, :]).astype(jnp.int32)
    rank = jnp.sum(jnp.cumsum(onehots, axis=0) * onehots, axis=1) - 1
    slot = target * cap + rank
    size = n_groups * cap

    def send(x, fill):
        full = jnp.full((size,) + x.shape[1:], fill, x.dtype).at[slot].set(x)
        full = full.reshape((n_groups, cap) + x.shape[1:])
        got = lax.all_to_all(full, GROUP_AXES, split_axis=0, concat_axis=0, tiled=True)
        return got.reshape((size,) + x.shape[1:])

    mine, ids, labels = send(unit, 0), send(global_id, -1), send(cluster, -1)

    def of_all(x):
        turns = [[(i, (i + by) % 4) for i in range(4)] for by in range(1, 4)]
        return jnp.concatenate([x] + [lax.ppermute(x, "x", turn) for turn in turns], axis=0)

    rows4, ids4, labels4 = of_all(mine), of_all(ids), of_all(labels)
    prod = jnp.einsum("id,jd->ij", mine, rows4, preferred_element_type=F32)
    keep = (labels[:, None] == labels4[None, :]) & (ids4[None, :] < ids[:, None])
    best = jnp.maximum(-1.0, jnp.max(jnp.where(keep, prod, -1.0), axis=1))
    back = lax.all_to_all(
        best.reshape(n_groups, cap), GROUP_AXES, split_axis=0, concat_axis=0, tiled=True
    )
    return back.reshape(size)[slot]


def by_devices(packed, ends):
    blocks = packed.reshape(CHIPS, CAP, WIDTH)
    got = lax.all_to_all(blocks, CHIP_AXES, split_axis=0, concat_axis=0, tiled=True)
    best = call(
        pairs_kernel, shape(DEVS, 128), got.reshape(SLOTS, WIDTH), ends
    )
    return best


def body(embeddings, owner, local_cluster):
    hist, ids = call(
        count_kernel,
        (shape(DEVS, 4, 128), shape(8, ROWS, dtype=jnp.int32)),
        owner.reshape(1, ROWS),
        local_cluster.reshape(ROWS // 128, 128),
        out_specs=(HBM, pl.BlockSpec()),
        scratch_shapes=[pltpu.VMEM((DEVS, 4, 128), F32), pltpu.SemaphoreType.DMA],
    )
    swap = [(0, 1), (1, 0)]
    ids2 = lax.ppermute(ids, "core", swap)
    hists = lax.all_to_all(hist, ALL, split_axis=0, concat_axis=0, tiled=True)
    embeddings2 = lax.ppermute(embeddings, "core", swap)
    packed, ends, places, load = call(
        place_kernel,
        (
            shape(SLOTS, WIDTH, dtype=BF16),
            shape(CHIPS, 8),
            shape(8, ROWS, dtype=jnp.int32),
            shape(1, 1, dtype=jnp.int32),
        ),
        hists, ids, ids2, embeddings, embeddings2,
        in_specs=[pl.BlockSpec()] * 3 + [ANY] * 2,
        scratch_shapes=[
            pltpu.VMEM((2 * ROWS, WIDTH), BF16),
            pltpu.SemaphoreType.DMA((2, ROWS // PIECE)),
        ],
    )
    best = by_devices(packed, ends)
    back = lax.all_to_all(best, ALL, split_axis=0, concat_axis=0, tiled=True)
    return lax.cond(
        load.reshape(()) <= CAP,
        lambda: call(home_kernel, shape(ROWS // 128, 128), back, places).reshape(ROWS),
        lambda: by_groups(embeddings, owner, local_cluster),
    )


def solution(mesh):
    fine = Mesh(mesh.devices.reshape(4, 4, 2, 4), ALL)
    return jax.shard_map(
        body,
        mesh=fine,
        in_specs=(P(ALL, None), P(ALL, None), P(ALL)),
        out_specs=P(ALL),
        check_vma=False,
    )
```

```python
import itertools
import math

import jax
import jax.numpy as jnp
from jax import lax
from jax.experimental import pallas as pl
from jax.experimental.pallas import tpu as pltpu
from jax.sharding import Mesh, PartitionSpec as P

CPG = 16
GROUPS = 32
CLUSTERS = GROUPS * CPG
ROWS = 768
WIDTH = 1024
CHIPS = 64
DEVS = 128
CAP = 24
SLOTS = CHIPS * CAP
LINE = 4 * CAP
PIECE = 128
ALL = ("z", "y", "core", "x")
GROUP_AXES = ("z", "y", "core")
CHIP_AXES = ("z", "y", "x")
ORDERS = tuple(itertools.permutations(range(4)))
BF16 = jnp.bfloat16
ANY = pl.BlockSpec(memory_space=pl.ANY)
HBM = pl.BlockSpec(memory_space=pltpu.HBM)
F32 = jnp.float32


def iota(shape, dim):
    return lax.broadcasted_iota(jnp.int32, shape, dim)


def dot(a, b, ca=1, cb=0):
    return lax.dot_general(a, b, (((ca,), (cb,)), ((), ())), preferred_element_type=F32)


def onehot(cond):
    return jnp.where(cond, 1.0, 0.0).astype(BF16)


def place():
    zy = lax.axis_index("z") * 4 + lax.axis_index("y")
    return lax.axis_index("core"), zy * 4 + lax.axis_index("x")


def count_kernel(owner_ref, local_ref, hist_ref, ids_ref, hists, sem):
    owner = owner_ref[...]
    local = jnp.concatenate([local_ref[j : j + 1, :] for j in range(ROWS // 128)], axis=1)
    by_owner = onehot(owner == iota((GROUPS, ROWS), 0))
    by_local = onehot(local == iota((CPG, ROWS), 0))
    pairs = dot(by_owner, by_local, 1, 1).astype(BF16)
    spread = onehot(iota((CPG, CLUSTERS), 1) % CPG == iota((CPG, CLUSTERS), 0))
    wide = dot(pairs, spread)
    mine = iota((GROUPS, CLUSTERS), 1) // CPG == iota((GROUPS, CLUSTERS), 0)
    counts = jnp.sum(jnp.where(mine, wide, 0.0), axis=0, keepdims=True)
    for j in range(CLUSTERS // 128):
        part = counts[:, j * 128 : (j + 1) * 128]
        hists[:, j, :] = jnp.broadcast_to(part, (DEVS, 128))
    leave = pltpu.make_async_copy(hists, hist_ref, sem)
    leave.start()
    cluster = owner * CPG + local
    eye = iota((128, 128), 0) == iota((128, 128), 1)
    rank = jnp.zeros((1, ROWS), jnp.int32)
    for j in range(ROWS // 128):
        part = jnp.broadcast_to(cluster[:, j * 128 : (j + 1) * 128], (128, 128))
        column = jnp.sum(jnp.where(eye, part, 0), axis=1, keepdims=True)
        width = ROWS - j * 128
        later = iota((128, width), 1) > iota((128, width), 0)
        hit = jnp.where((column == cluster[:, j * 128 :]) & later, 1, 0)
        found = jnp.sum(hit, axis=0, keepdims=True)
        if j:
            found = jnp.concatenate([jnp.zeros((1, j * 128), jnp.int32), found], axis=1)
        rank = rank + found
    which = iota((8, ROWS), 0)
    ids_ref[...] = jnp.where(which == 0, cluster, jnp.where(which == 1, rank, 0))
    leave.wait()


def wide_row(row):
    return jnp.broadcast_to(row.astype(F32), (8, row.shape[1])).astype(BF16)


def parity(cluster):
    return cluster & 1


def rotate(value, by, run=16):
    if by == 0:
        return value
    inside = (iota(value.shape, 1) & (run - 1)) >= by
    return jnp.where(inside, pltpu.roll(value, by, 1), pltpu.roll(value, by + 128 - run, 1))


def settle(base, parts):
    turned = [[rotate(part, r, 4) for r in range(4)] for part in parts]
    tops = [
        jnp.concatenate([jnp.max(base + t[r], axis=0, keepdims=True) for t in turned], axis=0)
        for r in range(4)
    ]
    lane4 = iota(tops[0].shape, 1) & 3
    best = turn = None
    for order in ORDERS:
        turns = [(j - order[j]) & 3 for j in range(4)]
        load, spin = tops[turns[3]], jnp.full(tops[0].shape, turns[3], jnp.int32)
        for j in range(3):
            load = jnp.where(lane4 == j, tops[turns[j]], load)
            spin = jnp.where(lane4 == j, turns[j], spin)
        load = jnp.maximum(load, rotate(load, 1, 4))
        load = jnp.maximum(load, rotate(load, 2, 4))
        if best is None:
            best, turn = load, spin
        else:
            turn = jnp.where(load < best, spin, turn)
            best = jnp.minimum(load, best)
    return best, turn, turned


def placing(parts, carried):
    base, placed = parts[0], [carried[0]]
    for part, rows in zip(parts[1:3], carried[1:3]):
        _, turn, (turned,) = settle(base, [part])
        base = base + spun(turned, turn)
        placed.append(spun([rotate(rows, r, 4) for r in range(4)], turn))
    loads, turns, _ = settle(base, [rotate(parts[3], 2 * c, 8) for c in range(4)])
    loads = jnp.maximum(loads, rotate(loads, 4, 8))
    best, turn, by = loads[0:1], turns[0:1], jnp.zeros((1, 128), jnp.int32)
    for c in range(1, 4):
        better = loads[c : c + 1] < best
        best = jnp.where(better, loads[c : c + 1], best)
        turn = jnp.where(better, turns[c : c + 1], turn)
        by = jnp.where(better, c, by)
    rows = spun([rotate(carried[3], 2 * c, 8) for c in range(4)], by)
    placed.append(spun([rotate(rows, r, 4) for r in range(4)], turn))
    return jnp.max(best, axis=1, keepdims=True), placed


def spun(turned, turn):
    rows = turned[0]
    for r in range(1, 4):
        rows = jnp.where(turn == r, turned[r], rows)
    return rows


def column(weights, rows):
    rows = [row.astype(F32) for row in rows]
    rows = jnp.concatenate(rows + [jnp.zeros((8 - len(rows), rows[0].shape[1]), F32)], axis=0)
    which = iota((8, 128), 0)
    weight = jnp.zeros((8, 128), F32)
    for n, w in enumerate(weights):
        weight = jnp.where(which == n, float(w), weight)
    return dot(rows.astype(BF16), weight.astype(BF16), 0, 0)


def same(col, row):
    parts = [onehot(col == row[:, j * 128 : (j + 1) * 128]) for j in range(row.shape[1] // 128)]
    return jnp.concatenate(parts, axis=1)


def place_kernel(
    hist_ref, ids_ref, ids2_ref, emb_ref, emb2_ref, out_ref, ends_ref, rows_ref, load_ref, raw, sems
):
    core, chip = place()
    reads = [
        pltpu.make_async_copy(
            source.at[pl.ds(n * PIECE, PIECE), :],
            raw.at[pl.ds(i * ROWS + n * PIECE, PIECE), :],
            sems.at[i, n],
        )
        for n in range(ROWS // PIECE)
        for i, source in enumerate((emb_ref, emb2_ref))
    ]
    for read in reads:
        read.start()
    hist = jnp.concatenate([hist_ref[:, j, :] for j in range(4)], axis=1)
    count0, count1 = hist[:CHIPS], hist[CHIPS:]
    both = (count0 + count1).astype(BF16)

    in_group = onehot((iota((GROUPS, CLUSTERS), 1) >> 4) == iota((GROUPS, CLUSTERS), 0))
    size_row = jnp.sum(dot(both, in_group, 1, 1), axis=0, keepdims=True)
    size_col = jnp.sum(dot(in_group, both, 1, 1), axis=1, keepdims=True)
    lower = iota((GROUPS, GROUPS), 0) < iota((GROUPS, GROUPS), 1)
    ahead = (size_col > size_row) | ((size_col == size_row) & lower)
    order = jnp.sum(jnp.where(ahead, 1.0, 0.0), axis=0, keepdims=True)
    order = dot(wide_row(order), in_group)[0:1].astype(jnp.int32)
    quarter = jnp.where(order < 16, order >> 3, 3 - (order & 1))
    octet = jnp.where(order < 8, order, jnp.where(order < 16, 15 - order, (31 - order) >> 1))
    local = iota((1, CLUSTERS), 1) & 15
    where = column((128, 16, 8, 1), (quarter, octet, local & 1, local >> 1))

    spread = same(where, iota((1, CLUSTERS), 1).astype(F32))
    names = (iota((8, CLUSTERS), 1) >> 4, iota((8, CLUSTERS), 1) & 15)
    names = jnp.where(iota((8, CLUSTERS), 0) == 0, *names).astype(F32)
    wide = dot(jnp.concatenate([count0, count1, names], axis=0).astype(BF16), spread)
    quarters = [wide[:, p * 128 : (p + 1) * 128] for p in range(4)]
    load, placed = placing([w[:CHIPS] + w[CHIPS:DEVS] for w in quarters], quarters)
    load_ref[...] = load.astype(jnp.int32)
    placed = jnp.concatenate(placed, axis=1)
    count0, count1, names = placed[:CHIPS], placed[CHIPS:DEVS], placed[DEVS:].astype(jnp.int32)
    at = iota((CLUSTERS, 8), 0)
    upto = iota((CLUSTERS, 8), 1)
    mine = (at & 127) == (chip >> 3) * 16 + core * 8 + (chip & 7)
    ends_ref[...] = dot(
        count0.astype(BF16), onehot(mine & ((at >> 7) * 2 <= upto))
    ) + dot(count1.astype(BF16), onehot(mine & ((at >> 7) * 2 + 1 <= upto)))

    here = iota((CHIPS, CLUSTERS), 0) == chip
    own0 = jnp.sum(jnp.where(here, count0, 0.0), axis=0, keepdims=True)
    own1 = jnp.sum(jnp.where(here, count1, 0.0), axis=0, keepdims=True)
    own = own0 + own1
    start = [jnp.zeros((1, 128), F32)]
    for p in range(3):
        start.append(start[-1] + own[:, p * 128 : (p + 1) * 128])
    start0 = jnp.concatenate(start, axis=1)
    start1 = start0 + own0
    device_row = (iota((1, CLUSTERS), 1) & 127).astype(F32)
    by_group = jnp.where(names[0:1] == iota((GROUPS, CLUSTERS), 0), 1.0, 0.0)
    by_local = onehot(names[1:2] == iota((CPG, CLUSTERS), 0))

    def table(row):
        return dot(by_local, (by_group * row).astype(BF16), 1, 1).astype(BF16)

    to_table, table0, table1 = table(device_row), table(start0), table(start1)

    def slots(ids, start):
        group = onehot((ids[0:1] >> 4) == iota((GROUPS, ROWS), 0))
        local = (ids[0:1] & 15) == iota((CPG, ROWS), 0)

        def look(table):
            return jnp.sum(jnp.where(local, dot(table, group), 0.0), axis=0, keepdims=True).astype(jnp.int32)

        to = look(to_table)
        k = look(start) + ids[1:2]
        return to, k, jnp.where(((to >> 3) & 1) == core, ((to >> 4) * 8 + (to & 7)) * CAP + k, -1)

    to, k, slot = slots(ids_ref[...], jnp.where(core == 0, table0, table1))
    _, _, slot2 = slots(ids2_ref[...], jnp.where(core == 0, table1, table0))
    rows_ref[...] = jnp.concatenate([to, k, jnp.zeros((6, ROWS), jnp.int32)], axis=0)
    slot = jnp.concatenate([slot, slot2], axis=1)
    for read in reads:
        read.wait()
    tile = 256
    at = iota((tile, 2 * ROWS), 0).astype(F32).astype(BF16)
    for n in range(SLOTS // tile):
        pick = jnp.clip(slot - n * tile, -1, tile).astype(F32).astype(BF16)
        rows = dot(jnp.where(pick == at, BF16(1), BF16(0)), raw[...])
        scale = lax.rsqrt(jnp.mean(rows * rows, axis=1, keepdims=True) + 1e-06) / math.sqrt(WIDTH)
        out_ref[n * tile : (n + 1) * tile, :] = (rows * scale).astype(BF16)


def moved(values, picks, *dims):
    total = None
    for _ in range(3):
        part = values.astype(BF16)
        values = values - part.astype(F32)
        product = dot(part, picks, *dims)
        total = product if total is None else total + product
    return total


def pairs_kernel(rows_ref, ends_ref, out_ref):
    at = iota((1, SLOTS), 1)
    chip = at * 2731 >> 16
    k = at - chip * CAP
    own_chip = chip == iota((CHIPS, SLOTS), 0)
    ends = dot(ends_ref[...].astype(BF16), onehot(own_chip), 0, 0)
    past = jnp.sum(jnp.where(k.astype(F32) >= ends, 1, 0), axis=0, keepdims=True)
    label = past >> 1
    dev = (chip >> 2) * 8 + (past & 1) * 4 + (chip & 3)
    label_col = column((1,), (label,))
    order_col = column((32, 1), (dev, k))
    label_row = label.astype(F32)
    order_row = (dev * 32 + k).astype(F32)
    best = []
    for low in range(0, SLOTS, 256):
        mine = slice(low, low + 256)
        sure, end = low // LINE * LINE, -(-(low + 256) // LINE) * LINE
        top = jnp.full((1, 256), -1.0, F32)
        for first, last in ((0, sure), (sure, end)):
            if first == last:
                continue
            other = slice(first, last)
            score = dot(rows_ref[other, :], rows_ref[mine, :], 1, 1)
            tops = []
            for c in range(2):
                part = slice(low + c * 128, low + (c + 1) * 128)
                keep = label_col[other] == label_row[:, part]
                if first == sure:
                    keep = keep & (order_col[other] < order_row[:, part])
                part = jnp.where(keep, score[:, c * 128 : (c + 1) * 128], -1.0)
                tops.append(jnp.max(part, axis=0, keepdims=True))
            top = jnp.maximum(top, jnp.concatenate(tops, axis=1))
        best.append(top)
    best = jnp.concatenate(best, axis=1)
    block = jnp.where(own_chip, best, 0.0)
    at = iota((SLOTS, 128), 0)
    place_col = at - (at * 2731 >> 16) * CAP == iota((SLOTS, 128), 1)
    found = moved(block, onehot(place_col))
    for n in range(DEVS // 8):
        four = found[n * 4 : (n + 1) * 4, :]
        out_ref[n * 8 : (n + 1) * 8, :] = jnp.concatenate([four, four], axis=0)


def home_kernel(got_ref, rows_ref, out_ref):
    to, k = rows_ref[0:1, :], rows_ref[1:2, :]
    chip = (to >> 4) * 8 + (to & 7)
    dev = (chip >> 2) * 8 + ((to >> 3) & 1) * 4 + (chip & 3)
    cand = moved(got_ref[:, 0:32], onehot(dev == iota((DEVS, ROWS), 0)), 0, 0)
    best = jnp.sum(jnp.where(k == iota((32, ROWS), 0), cand, 0.0), axis=0, keepdims=True)
    for j in range(ROWS // 128):
        out_ref[j : j + 1, :] = best[:, j * 128 : (j + 1) * 128]


def call(kernel, out_shape, *args, vmem=32 * 2**20, **kwargs):
    return pl.pallas_call(
        kernel,
        out_shape=out_shape,
        compiler_params=pltpu.CompilerParams(vmem_limit_bytes=vmem),
        **kwargs,
    )(*args)


def shape(*dims, dtype=F32):
    return jax.ShapeDtypeStruct(dims, dtype)


def by_groups(embeddings, owner, local_cluster):
    rows, width = embeddings.shape
    n_groups = GROUPS
    cap = 2 * rows // n_groups
    emb32 = embeddings.astype(F32)
    scale = lax.rsqrt(jnp.mean(emb32 * emb32, axis=1, keepdims=True) + 1e-06) / math.sqrt(width)
    unit = (emb32 * scale).astype(BF16)
    target = owner[:, 0]
    cluster = target * CPG + local_cluster
    device = lax.axis_index(ALL)
    global_id = device * rows + jnp.arange(rows, dtype=jnp.int32)
    onehots = (target[:, None] == jnp.arange(n_groups, dtype=jnp.int32)[None, :]).astype(jnp.int32)
    rank = jnp.sum(jnp.cumsum(onehots, axis=0) * onehots, axis=1) - 1
    slot = target * cap + rank
    size = n_groups * cap

    def send(x, fill):
        full = jnp.full((size,) + x.shape[1:], fill, x.dtype).at[slot].set(x)
        full = full.reshape((n_groups, cap) + x.shape[1:])
        got = lax.all_to_all(full, GROUP_AXES, split_axis=0, concat_axis=0, tiled=True)
        return got.reshape((size,) + x.shape[1:])

    mine, ids, labels = send(unit, 0), send(global_id, -1), send(cluster, -1)

    def of_all(x):
        turns = [[(i, (i + by) % 4) for i in range(4)] for by in range(1, 4)]
        return jnp.concatenate([x] + [lax.ppermute(x, "x", turn) for turn in turns], axis=0)

    rows4, ids4, labels4 = of_all(mine), of_all(ids), of_all(labels)
    prod = jnp.einsum("id,jd->ij", mine, rows4, preferred_element_type=F32)
    keep = (labels[:, None] == labels4[None, :]) & (ids4[None, :] < ids[:, None])
    best = jnp.maximum(-1.0, jnp.max(jnp.where(keep, prod, -1.0), axis=1))
    back = lax.all_to_all(
        best.reshape(n_groups, cap), GROUP_AXES, split_axis=0, concat_axis=0, tiled=True
    )
    return back.reshape(size)[slot]


def by_devices(packed, ends):
    blocks = packed.reshape(CHIPS, CAP, WIDTH)
    got = lax.all_to_all(blocks, CHIP_AXES, split_axis=0, concat_axis=0, tiled=True)
    best = call(
        pairs_kernel, shape(DEVS, 128), got.reshape(SLOTS, WIDTH), ends
    )
    return best


def body(embeddings, owner, local_cluster):
    hist, ids = call(
        count_kernel,
        (shape(DEVS, 4, 128), shape(8, ROWS, dtype=jnp.int32)),
        owner.reshape(1, ROWS),
        local_cluster.reshape(ROWS // 128, 128),
        out_specs=(HBM, pl.BlockSpec()),
        scratch_shapes=[pltpu.VMEM((DEVS, 4, 128), F32), pltpu.SemaphoreType.DMA],
    )
    swap = [(0, 1), (1, 0)]
    ids2 = lax.ppermute(ids, "core", swap)
    hists = lax.all_to_all(hist, ("core",) + CHIP_AXES, split_axis=0, concat_axis=0, tiled=True)
    embeddings2 = lax.ppermute(embeddings, "core", swap)
    packed, ends, places, load = call(
        place_kernel,
        (
            shape(SLOTS, WIDTH, dtype=BF16),
            shape(CHIPS, 8),
            shape(8, ROWS, dtype=jnp.int32),
            shape(1, 1, dtype=jnp.int32),
        ),
        hists, ids, ids2, embeddings, embeddings2,
        in_specs=[pl.BlockSpec()] * 3 + [ANY] * 2,
        scratch_shapes=[
            pltpu.VMEM((2 * ROWS, WIDTH), BF16),
            pltpu.SemaphoreType.DMA((2, ROWS // PIECE)),
        ],
    )
    best = by_devices(packed, ends)
    back = lax.all_to_all(best, ALL, split_axis=0, concat_axis=0, tiled=True)
    return lax.cond(
        load.reshape(()) <= CAP,
        lambda: call(home_kernel, shape(ROWS // 128, 128), back, places).reshape(ROWS),
        lambda: by_groups(embeddings, owner, local_cluster),
    )


def solution(mesh):
    fine = Mesh(mesh.devices.reshape(4, 4, 2, 4), ALL)
    return jax.shard_map(
        body,
        mesh=fine,
        in_specs=(P(ALL, None), P(ALL, None), P(ALL)),
        out_specs=P(ALL),
        check_vma=False,
    )
```

```python
import itertools
import math

import jax
import jax.numpy as jnp
from jax import lax
from jax.experimental import pallas as pl
from jax.experimental.pallas import tpu as pltpu
from jax.sharding import Mesh, PartitionSpec as P

CPG = 16
GROUPS = 32
CLUSTERS = GROUPS * CPG
ROWS = 768
WIDTH = 1024
CHIPS = 64
DEVS = 128
CAP = 24
SLOTS = CHIPS * CAP
LINE = 4 * CAP
PIECE = 768
ALL = ("z", "y", "core", "x")
GROUP_AXES = ("z", "y", "core")
CHIP_AXES = ("z", "y", "x")
ORDERS = tuple(itertools.permutations(range(4)))
BF16 = jnp.bfloat16
ANY = pl.BlockSpec(memory_space=pl.ANY)
HBM = pl.BlockSpec(memory_space=pltpu.HBM)
F32 = jnp.float32


def iota(shape, dim):
    return lax.broadcasted_iota(jnp.int32, shape, dim)


def dot(a, b, ca=1, cb=0):
    return lax.dot_general(a, b, (((ca,), (cb,)), ((), ())), preferred_element_type=F32)


def onehot(cond):
    return jnp.where(cond, 1.0, 0.0).astype(BF16)


def place():
    zy = lax.axis_index("z") * 4 + lax.axis_index("y")
    return lax.axis_index("core"), zy * 4 + lax.axis_index("x")


def count_kernel(owner_ref, local_ref, hist_ref, ids_ref, hists, sem):
    owner = owner_ref[...]
    local = jnp.concatenate([local_ref[j : j + 1, :] for j in range(ROWS // 128)], axis=1)
    by_owner = onehot(owner == iota((GROUPS, ROWS), 0))
    by_local = onehot(local == iota((CPG, ROWS), 0))
    pairs = dot(by_owner, by_local, 1, 1).astype(BF16)
    spread = onehot(iota((CPG, CLUSTERS), 1) % CPG == iota((CPG, CLUSTERS), 0))
    wide = dot(pairs, spread)
    mine = iota((GROUPS, CLUSTERS), 1) // CPG == iota((GROUPS, CLUSTERS), 0)
    counts = jnp.sum(jnp.where(mine, wide, 0.0), axis=0, keepdims=True)
    for j in range(CLUSTERS // 128):
        part = counts[:, j * 128 : (j + 1) * 128]
        hists[:, j, :] = jnp.broadcast_to(part, (DEVS, 128))
    leave = pltpu.make_async_copy(hists, hist_ref, sem)
    leave.start()
    cluster = owner * CPG + local
    eye = iota((128, 128), 0) == iota((128, 128), 1)
    rank = jnp.zeros((1, ROWS), jnp.int32)
    for j in range(ROWS // 128):
        part = jnp.broadcast_to(cluster[:, j * 128 : (j + 1) * 128], (128, 128))
        column = jnp.sum(jnp.where(eye, part, 0), axis=1, keepdims=True)
        width = ROWS - j * 128
        later = iota((128, width), 1) > iota((128, width), 0)
        hit = jnp.where((column == cluster[:, j * 128 :]) & later, 1, 0)
        found = jnp.sum(hit, axis=0, keepdims=True)
        if j:
            found = jnp.concatenate([jnp.zeros((1, j * 128), jnp.int32), found], axis=1)
        rank = rank + found
    which = iota((8, ROWS), 0)
    ids_ref[...] = jnp.where(which == 0, cluster, jnp.where(which == 1, rank, 0))
    leave.wait()


def wide_row(row):
    return jnp.broadcast_to(row.astype(F32), (8, row.shape[1])).astype(BF16)


def parity(cluster):
    return cluster & 1


def rotate(value, by, run=16):
    if by == 0:
        return value
    inside = (iota(value.shape, 1) & (run - 1)) >= by
    return jnp.where(inside, pltpu.roll(value, by, 1), pltpu.roll(value, by + 128 - run, 1))


def settle(base, parts):
    turned = [[rotate(part, r, 4) for r in range(4)] for part in parts]
    tops = [
        jnp.concatenate([jnp.max(base + t[r], axis=0, keepdims=True) for t in turned], axis=0)
        for r in range(4)
    ]
    lane4 = iota(tops[0].shape, 1) & 3
    best = turn = None
    for order in ORDERS:
        turns = [(j - order[j]) & 3 for j in range(4)]
        load, spin = tops[turns[3]], jnp.full(tops[0].shape, turns[3], jnp.int32)
        for j in range(3):
            load = jnp.where(lane4 == j, tops[turns[j]], load)
            spin = jnp.where(lane4 == j, turns[j], spin)
        load = jnp.maximum(load, rotate(load, 1, 4))
        load = jnp.maximum(load, rotate(load, 2, 4))
        if best is None:
            best, turn = load, spin
        else:
            turn = jnp.where(load < best, spin, turn)
            best = jnp.minimum(load, best)
    return best, turn, turned


def placing(parts, carried):
    base, placed = parts[0], [carried[0]]
    for part, rows in zip(parts[1:3], carried[1:3]):
        _, turn, (turned,) = settle(base, [part])
        base = base + spun(turned, turn)
        placed.append(spun([rotate(rows, r, 4) for r in range(4)], turn))
    loads, turns, _ = settle(base, [rotate(parts[3], 2 * c, 8) for c in range(4)])
    loads = jnp.maximum(loads, rotate(loads, 4, 8))
    best, turn, by = loads[0:1], turns[0:1], jnp.zeros((1, 128), jnp.int32)
    for c in range(1, 4):
        better = loads[c : c + 1] < best
        best = jnp.where(better, loads[c : c + 1], best)
        turn = jnp.where(better, turns[c : c + 1], turn)
        by = jnp.where(better, c, by)
    rows = spun([rotate(carried[3], 2 * c, 8) for c in range(4)], by)
    placed.append(spun([rotate(rows, r, 4) for r in range(4)], turn))
    return jnp.max(best, axis=1, keepdims=True), placed


def spun(turned, turn):
    rows = turned[0]
    for r in range(1, 4):
        rows = jnp.where(turn == r, turned[r], rows)
    return rows


def column(weights, rows):
    rows = [row.astype(F32) for row in rows]
    rows = jnp.concatenate(rows + [jnp.zeros((8 - len(rows), rows[0].shape[1]), F32)], axis=0)
    which = iota((8, 128), 0)
    weight = jnp.zeros((8, 128), F32)
    for n, w in enumerate(weights):
        weight = jnp.where(which == n, float(w), weight)
    return dot(rows.astype(BF16), weight.astype(BF16), 0, 0)


def same(col, row):
    parts = [onehot(col == row[:, j * 128 : (j + 1) * 128]) for j in range(row.shape[1] // 128)]
    return jnp.concatenate(parts, axis=1)


def place_kernel(
    hist_ref, ids_ref, ids2_ref, emb_ref, emb2_ref, out_ref, ends_ref, rows_ref, load_ref, raw, sems
):
    core, chip = place()
    reads = [
        pltpu.make_async_copy(
            source.at[pl.ds(n * PIECE, PIECE), :],
            raw.at[pl.ds(i * ROWS + n * PIECE, PIECE), :],
            sems.at[i, n],
        )
        for n in range(ROWS // PIECE)
        for i, source in enumerate((emb_ref, emb2_ref))
    ]
    for read in reads:
        read.start()
    hist = jnp.concatenate([hist_ref[:, j, :] for j in range(4)], axis=1)
    count0, count1 = hist[:CHIPS], hist[CHIPS:]
    both = (count0 + count1).astype(BF16)

    in_group = onehot((iota((GROUPS, CLUSTERS), 1) >> 4) == iota((GROUPS, CLUSTERS), 0))
    size_row = jnp.sum(dot(both, in_group, 1, 1), axis=0, keepdims=True)
    size_col = jnp.sum(dot(in_group, both, 1, 1), axis=1, keepdims=True)
    lower = iota((GROUPS, GROUPS), 0) < iota((GROUPS, GROUPS), 1)
    ahead = (size_col > size_row) | ((size_col == size_row) & lower)
    order = jnp.sum(jnp.where(ahead, 1.0, 0.0), axis=0, keepdims=True)
    order = dot(wide_row(order), in_group)[0:1].astype(jnp.int32)
    quarter = jnp.where(order < 16, order >> 3, 3 - (order & 1))
    octet = jnp.where(order < 8, order, jnp.where(order < 16, 15 - order, (31 - order) >> 1))
    local = iota((1, CLUSTERS), 1) & 15
    where = column((128, 16, 8, 1), (quarter, octet, local & 1, local >> 1))

    spread = same(where, iota((1, CLUSTERS), 1).astype(F32))
    names = (iota((8, CLUSTERS), 1) >> 4, iota((8, CLUSTERS), 1) & 15)
    names = jnp.where(iota((8, CLUSTERS), 0) == 0, *names).astype(F32)
    wide = dot(jnp.concatenate([count0, count1, names], axis=0).astype(BF16), spread)
    quarters = [wide[:, p * 128 : (p + 1) * 128] for p in range(4)]
    load, placed = placing([w[:CHIPS] + w[CHIPS:DEVS] for w in quarters], quarters)
    load_ref[...] = load.astype(jnp.int32)
    placed = jnp.concatenate(placed, axis=1)
    count0, count1, names = placed[:CHIPS], placed[CHIPS:DEVS], placed[DEVS:].astype(jnp.int32)
    at = iota((CLUSTERS, 8), 0)
    upto = iota((CLUSTERS, 8), 1)
    mine = (at & 127) == (chip >> 3) * 16 + core * 8 + (chip & 7)
    ends_ref[...] = dot(
        count0.astype(BF16), onehot(mine & ((at >> 7) * 2 <= upto))
    ) + dot(count1.astype(BF16), onehot(mine & ((at >> 7) * 2 + 1 <= upto)))

    here = iota((CHIPS, CLUSTERS), 0) == chip
    own0 = jnp.sum(jnp.where(here, count0, 0.0), axis=0, keepdims=True)
    own1 = jnp.sum(jnp.where(here, count1, 0.0), axis=0, keepdims=True)
    own = own0 + own1
    start = [jnp.zeros((1, 128), F32)]
    for p in range(3):
        start.append(start[-1] + own[:, p * 128 : (p + 1) * 128])
    start0 = jnp.concatenate(start, axis=1)
    start1 = start0 + own0
    device_row = (iota((1, CLUSTERS), 1) & 127).astype(F32)
    by_group = jnp.where(names[0:1] == iota((GROUPS, CLUSTERS), 0), 1.0, 0.0)
    by_local = onehot(names[1:2] == iota((CPG, CLUSTERS), 0))

    def table(row):
        return dot(by_local, (by_group * row).astype(BF16), 1, 1).astype(BF16)

    to_table, table0, table1 = table(device_row), table(start0), table(start1)

    def slots(ids, start):
        group = onehot((ids[0:1] >> 4) == iota((GROUPS, ROWS), 0))
        local = (ids[0:1] & 15) == iota((CPG, ROWS), 0)

        def look(table):
            return jnp.sum(jnp.where(local, dot(table, group), 0.0), axis=0, keepdims=True).astype(jnp.int32)

        to = look(to_table)
        k = look(start) + ids[1:2]
        return to, k, jnp.where(((to >> 3) & 1) == core, ((to >> 4) * 8 + (to & 7)) * CAP + k, -1)

    to, k, slot = slots(ids_ref[...], jnp.where(core == 0, table0, table1))
    _, _, slot2 = slots(ids2_ref[...], jnp.where(core == 0, table1, table0))
    rows_ref[...] = jnp.concatenate([to, k, jnp.zeros((6, ROWS), jnp.int32)], axis=0)
    slot = jnp.concatenate([slot, slot2], axis=1)
    for read in reads:
        read.wait()
    tile = 256
    at = iota((tile, 2 * ROWS), 0).astype(F32).astype(BF16)
    for n in range(SLOTS // tile):
        pick = jnp.clip(slot - n * tile, -1, tile).astype(F32).astype(BF16)
        rows = dot(jnp.where(pick == at, BF16(1), BF16(0)), raw[...])
        scale = lax.rsqrt(jnp.mean(rows * rows, axis=1, keepdims=True) + 1e-06) / math.sqrt(WIDTH)
        out_ref[n * tile : (n + 1) * tile, :] = (rows * scale).astype(BF16)


def moved(values, picks, *dims):
    total = None
    for _ in range(3):
        part = values.astype(BF16)
        values = values - part.astype(F32)
        product = dot(part, picks, *dims)
        total = product if total is None else total + product
    return total


def pairs_kernel(rows_ref, ends_ref, out_ref):
    at = iota((1, SLOTS), 1)
    chip = at * 2731 >> 16
    k = at - chip * CAP
    own_chip = chip == iota((CHIPS, SLOTS), 0)
    ends = dot(ends_ref[...].astype(BF16), onehot(own_chip), 0, 0)
    past = jnp.sum(jnp.where(k.astype(F32) >= ends, 1, 0), axis=0, keepdims=True)
    label = past >> 1
    dev = (chip >> 2) * 8 + (past & 1) * 4 + (chip & 3)
    label_col = column((1,), (label,))
    order_col = column((32, 1), (dev, k))
    label_row = label.astype(F32)
    order_row = (dev * 32 + k).astype(F32)
    best = []
    for low in range(0, SLOTS, 256):
        mine = slice(low, low + 256)
        sure, end = low // LINE * LINE, -(-(low + 256) // LINE) * LINE
        top = jnp.full((1, 256), -1.0, F32)
        for first, last in ((0, sure), (sure, end)):
            if first == last:
                continue
            other = slice(first, last)
            score = dot(rows_ref[other, :], rows_ref[mine, :], 1, 1)
            tops = []
            for c in range(2):
                part = slice(low + c * 128, low + (c + 1) * 128)
                keep = label_col[other] == label_row[:, part]
                if first == sure:
                    keep = keep & (order_col[other] < order_row[:, part])
                part = jnp.where(keep, score[:, c * 128 : (c + 1) * 128], -1.0)
                tops.append(jnp.max(part, axis=0, keepdims=True))
            top = jnp.maximum(top, jnp.concatenate(tops, axis=1))
        best.append(top)
    best = jnp.concatenate(best, axis=1)
    block = jnp.where(own_chip, best, 0.0)
    at = iota((SLOTS, 128), 0)
    place_col = at - (at * 2731 >> 16) * CAP == iota((SLOTS, 128), 1)
    found = moved(block, onehot(place_col))
    for n in range(DEVS // 8):
        four = found[n * 4 : (n + 1) * 4, :]
        out_ref[n * 8 : (n + 1) * 8, :] = jnp.concatenate([four, four], axis=0)


def home_kernel(got_ref, rows_ref, out_ref):
    to, k = rows_ref[0:1, :], rows_ref[1:2, :]
    chip = (to >> 4) * 8 + (to & 7)
    dev = (chip >> 2) * 8 + ((to >> 3) & 1) * 4 + (chip & 3)
    cand = moved(got_ref[:, 0:32], onehot(dev == iota((DEVS, ROWS), 0)), 0, 0)
    best = jnp.sum(jnp.where(k == iota((32, ROWS), 0), cand, 0.0), axis=0, keepdims=True)
    for j in range(ROWS // 128):
        out_ref[j : j + 1, :] = best[:, j * 128 : (j + 1) * 128]


def call(kernel, out_shape, *args, vmem=32 * 2**20, **kwargs):
    return pl.pallas_call(
        kernel,
        out_shape=out_shape,
        compiler_params=pltpu.CompilerParams(vmem_limit_bytes=vmem),
        **kwargs,
    )(*args)


def shape(*dims, dtype=F32):
    return jax.ShapeDtypeStruct(dims, dtype)


def by_groups(embeddings, owner, local_cluster):
    rows, width = embeddings.shape
    n_groups = GROUPS
    cap = 2 * rows // n_groups
    emb32 = embeddings.astype(F32)
    scale = lax.rsqrt(jnp.mean(emb32 * emb32, axis=1, keepdims=True) + 1e-06) / math.sqrt(width)
    unit = (emb32 * scale).astype(BF16)
    target = owner[:, 0]
    cluster = target * CPG + local_cluster
    device = lax.axis_index(ALL)
    global_id = device * rows + jnp.arange(rows, dtype=jnp.int32)
    onehots = (target[:, None] == jnp.arange(n_groups, dtype=jnp.int32)[None, :]).astype(jnp.int32)
    rank = jnp.sum(jnp.cumsum(onehots, axis=0) * onehots, axis=1) - 1
    slot = target * cap + rank
    size = n_groups * cap

    def send(x, fill):
        full = jnp.full((size,) + x.shape[1:], fill, x.dtype).at[slot].set(x)
        full = full.reshape((n_groups, cap) + x.shape[1:])
        got = lax.all_to_all(full, GROUP_AXES, split_axis=0, concat_axis=0, tiled=True)
        return got.reshape((size,) + x.shape[1:])

    mine, ids, labels = send(unit, 0), send(global_id, -1), send(cluster, -1)

    def of_all(x):
        turns = [[(i, (i + by) % 4) for i in range(4)] for by in range(1, 4)]
        return jnp.concatenate([x] + [lax.ppermute(x, "x", turn) for turn in turns], axis=0)

    rows4, ids4, labels4 = of_all(mine), of_all(ids), of_all(labels)
    prod = jnp.einsum("id,jd->ij", mine, rows4, preferred_element_type=F32)
    keep = (labels[:, None] == labels4[None, :]) & (ids4[None, :] < ids[:, None])
    best = jnp.maximum(-1.0, jnp.max(jnp.where(keep, prod, -1.0), axis=1))
    back = lax.all_to_all(
        best.reshape(n_groups, cap), GROUP_AXES, split_axis=0, concat_axis=0, tiled=True
    )
    return back.reshape(size)[slot]


def by_devices(packed, ends):
    blocks = packed.reshape(CHIPS, CAP, WIDTH)
    got = lax.all_to_all(blocks, CHIP_AXES, split_axis=0, concat_axis=0, tiled=True)
    best = call(
        pairs_kernel, shape(DEVS, 128), got.reshape(SLOTS, WIDTH), ends
    )
    return best


def body(embeddings, owner, local_cluster):
    hist, ids = call(
        count_kernel,
        (shape(DEVS, 4, 128), shape(8, ROWS, dtype=jnp.int32)),
        owner.reshape(1, ROWS),
        local_cluster.reshape(ROWS // 128, 128),
        out_specs=(HBM, pl.BlockSpec()),
        scratch_shapes=[pltpu.VMEM((DEVS, 4, 128), F32), pltpu.SemaphoreType.DMA],
    )
    swap = [(0, 1), (1, 0)]
    ids2 = lax.ppermute(ids, "core", swap)
    hists = lax.all_to_all(hist, ("core",) + CHIP_AXES, split_axis=0, concat_axis=0, tiled=True)
    embeddings2 = lax.ppermute(embeddings, "core", swap)
    packed, ends, places, load = call(
        place_kernel,
        (
            shape(SLOTS, WIDTH, dtype=BF16),
            shape(CHIPS, 8),
            shape(8, ROWS, dtype=jnp.int32),
            shape(1, 1, dtype=jnp.int32),
        ),
        hists, ids, ids2, embeddings, embeddings2,
        in_specs=[pl.BlockSpec()] * 3 + [ANY] * 2,
        scratch_shapes=[
            pltpu.VMEM((2 * ROWS, WIDTH), BF16),
            pltpu.SemaphoreType.DMA((2, ROWS // PIECE)),
        ],
    )
    best = by_devices(packed, ends)
    back = lax.all_to_all(best, ALL, split_axis=0, concat_axis=0, tiled=True)
    return lax.cond(
        load.reshape(()) <= CAP,
        lambda: call(home_kernel, shape(ROWS // 128, 128), back, places).reshape(ROWS),
        lambda: by_groups(embeddings, owner, local_cluster),
    )


def solution(mesh):
    fine = Mesh(mesh.devices.reshape(4, 4, 2, 4), ALL)
    return jax.shard_map(
        body,
        mesh=fine,
        in_specs=(P(ALL, None), P(ALL, None), P(ALL)),
        out_specs=P(ALL),
        check_vma=False,
    )
```
